32 devices in a mesh: group: 8 (over z, y), roll: 4 (over x, core).
Axes of the slice: x: 2, y: 2, z: 4, core: 2. Of those that a mesh axis runs over, the one named last changes fastest.
Arguments:
- prefix_latent: float32 [8192, 576], P(('group', 'roll')), parts along dimension 0, may hold values from -8 to 8
- suffix_latent: bfloat16 [256, 256, 576], P(('group', 'roll')), parts along dimension 0, may hold values from -8 to 8
- suffix_len: int32 [256], P(('group', 'roll')), parts along dimension 0, may hold values from 1 to 256, as said below
- new_latent: bfloat16 [256, 2, 576], P(('group', 'roll')), parts along dimension 0, may hold values from -8 to 8
- queries: bfloat16 [256, 2, 64, 576], P(('group', 'roll')), parts along dimension 0, may hold values from -8 to 8
- w_uv: bfloat16 [64, 512, 128], P('roll'), may hold values from -1 to 1
- w_out: bfloat16 [8192, 7168], P('roll'), may hold values from -0.25 to 0.25
Outputs:
- layer_out: bfloat16 [256, 2, 7168], P(('group', 'roll')), parts along dimension 0
The draws below stay inside these ranges and needn't reach their ends.
There are 8 independent parts, one for each index of `group`. The reference program is written for one: setup_inputs(seed, part) draws one part's arguments, and reference() takes and returns one part's arrays. A program takes and returns all parts, laid end to end along the dimension named above; an argument that names none is the same for every part. Nothing has to cross between parts.
Inputs may be any that keep to these rules, and one draw needn't show every extreme that they name: Row r uses the first suffix_len[r] positions of its suffix cache; in every draw some row has 256 and some row has 1.
All inputs are finite; a program needn't handle non-finite values.
Results may differ from the reference program's by a relative error of at most 0.012.
Values may be sent and summed in bfloat16 or wider, within the bound.
No kernel may reach another device: no remote copies, remote signals or barrier semaphores. Data moves between devices by JAX's collectives and lax.ppermute only.
A program may use at most 128 MiB of HBM per device.

```python
import jax
import jax.numpy as jnp
from jax import lax

D = 7168
LATENT = 512
ROPE = 64
HEAD_V = 128
QK_HEAD = 192
HEADS = 64
STEPS = 2
SUF = 256
PROMPT = 1024
ROWS = 32
N_ROLL = 4


def draw_prefix_latent(key, part):
    key = jax.random.fold_in(key, 3)
    full_shape = (PROMPT, LATENT + ROPE)
    values = jax.random.truncated_normal(key, -6.0, 6.0, full_shape, jnp.float32)
    return values


def draw_queries(key, part):
    key = jax.random.fold_in(key, 5)
    full_shape = (ROWS, STEPS, HEADS, LATENT + ROPE)
    values = jax.random.truncated_normal(key, -6.0, 6.0, full_shape, jnp.float32)
    return values.astype(jnp.bfloat16)


def draw_suffix_len(key, part):
    key = jax.random.fold_in(key, 7)
    key_first, key_second, key_order = jax.random.split(key, 3)
    first_draw = jax.random.randint(key_first, (ROWS,), 1, SUF + 1)
    second_draw = jax.random.randint(key_second, (ROWS,), 1, SUF + 1)
    lengths = jnp.minimum(first_draw, second_draw)
    row_order = jax.random.permutation(key_order, ROWS)
    lengths = lengths.at[row_order[0]].set(SUF).at[row_order[1]].set(1)
    return lengths.astype(jnp.int32)


def block_levels(rng, shape, cuts, least, high):
    level = 1.0
    for axis_at, shards_of in cuts:
        heights = jax.random.uniform(jax.random.fold_in(jax.random.fold_in(rng, 6), axis_at), (shards_of,), jnp.float32, least / len(cuts), high / len(cuts))
        level = level * jnp.repeat(jnp.exp(heights), shape[axis_at] // shards_of).reshape((-1,) + (1,) * (len(shape) - 1 - axis_at))
    return level


def normal_values(own_key, dims, deviation, reach, cuts=(), held_as=jnp.bfloat16):
    values = deviation * jax.random.normal(own_key, dims, jnp.float32)
    if cuts:
        values = values * block_levels(own_key, dims, cuts, -0.22, 0.18)
    return jnp.clip(values, -reach, reach).astype(held_as)


def setup_inputs(seed: int = 0, part: int = 0) -> dict:
    key_list = jax.random.split(jax.random.key(seed), 8)
    own_keys = jax.random.split(jax.random.fold_in(key_list[7], part), 8)
    return {
        "prefix_latent": draw_prefix_latent(jax.random.fold_in(jax.random.fold_in(key_list[7], part), 71), part),
        "suffix_latent": normal_values(own_keys[1], (ROWS, SUF, LATENT + ROPE), 1.4, 8.0, ((0, 4),)),
        "suffix_len": draw_suffix_len(jax.random.fold_in(jax.random.fold_in(key_list[7], part), 71), part),
        "new_latent": normal_values(own_keys[3], (ROWS, STEPS, LATENT + ROPE), 2.2, 8.0, ((0, 4),)),
        "queries": draw_queries(jax.random.fold_in(jax.random.fold_in(key_list[7], part), 71), part),
        "w_uv": normal_values(key_list[5], (HEADS, LATENT, HEAD_V), (LATENT // 16) ** -0.5, 1.0, ((0, 4),)),
        "w_out": normal_values(key_list[6], (HEADS * HEAD_V, D), (HEADS * HEAD_V // 16) ** -0.5, 0.25, ((0, 4),)),
    }


def reference(prefix_latent, suffix_latent, suffix_len, new_latent, queries, w_uv, w_out):
    prefix_keys = prefix_latent.astype(jnp.bfloat16)
    scaling = QK_HEAD ** -0.5
    positions = jnp.arange(PROMPT + SUF + STEPS, dtype=jnp.int32)
    step_ids = jnp.arange(STEPS, dtype=jnp.int32)
    uv_weight = w_uv.astype(jnp.float32)
    group_width = HEADS * HEAD_V // N_ROLL
    out_groups = w_out.astype(jnp.float32).reshape(N_ROLL, group_width, D)

    def one_row(items):
        query_row, suffix_row, new_row, row_length = items
        keys_all = jnp.concatenate([prefix_keys, suffix_row, new_row], axis=0)
        in_suffix = (positions >= PROMPT) & (positions < PROMPT + SUF)
        live_keys = jnp.where(in_suffix, positions - PROMPT < row_length, True)
        new_index = positions - PROMPT - SUF
        live_mask = jnp.where(positions[None, :] >= PROMPT + SUF, new_index[None, :] <= step_ids[:, None], live_keys[None, :])
        live_mask = live_mask[:, None, :]
        scores = jnp.einsum('shc,nc->shn', query_row.astype(jnp.float32), keys_all.astype(jnp.float32)) * scaling
        scores = jnp.where(live_mask, scores, -1e30)
        largest = jnp.max(scores, axis=-1, keepdims=True)
        weights = jnp.where(live_mask, jnp.exp(scores - largest), 0.0)
        total_sum = jnp.sum(weights, axis=-1)
        probs_bf = weights.astype(jnp.bfloat16)
        summed = jnp.einsum('shn,nc->shc', probs_bf.astype(jnp.float32), keys_all[:, :LATENT].astype(jnp.float32))
        attended = (summed / total_sum[..., None]).astype(jnp.bfloat16)
        head_out = jnp.einsum('shc,hcv->shv', attended.astype(jnp.float32), uv_weight).astype(jnp.bfloat16)
        flat_heads = head_out.reshape(STEPS, N_ROLL, group_width).astype(jnp.float32)
        partial_sums = jnp.einsum('sgk,gkd->gsd', flat_heads, out_groups).astype(jnp.bfloat16)
        partial_sums = lax.optimization_barrier(partial_sums)
        return jnp.sum(partial_sums.astype(jnp.float32), axis=0).astype(jnp.bfloat16)

    return lax.map(one_row, (queries, suffix_latent, new_latent, suffix_len))
```

```python
import functools
import math

import jax
import jax.numpy as jnp
from jax import lax
from jax.experimental import pallas as pl
from jax.experimental.pallas import tpu as pltpu
from jax.sharding import PartitionSpec as P

LATENT = 512
QK_HEAD = 192
SCALE2 = QK_HEAD**-0.5 * math.log2(math.e)
NEG = -1e30
CHUNK_HEADS = 4
OUT_PARTS = 2
MIB = 2**20


def dot_nt(a, b):
    return lax.dot_general(a, b, (((1,), (1,)), ((), ())), preferred_element_type=jnp.float32)


def dot_nn(a, b):
    return jnp.dot(a, b, preferred_element_type=jnp.float32)


def near_kernel(len_ref, q_ref, suf_ref, new_ref, *refs):
    key_refs, (m_ref, l_ref, acc_ref) = refs[:-3], refs[-3:]
    row = pl.program_id(0)
    steps, heads, width = q_ref.shape[1:]
    rows = steps * heads
    q = q_ref[0].reshape(rows, width)
    keys = [k[...] for k in key_refs] + [suf_ref[0]]
    scores = [dot_nn(q, k) for k in keys]
    at = lax.broadcasted_iota(jnp.int32, scores[-1].shape, 1)
    scores[-1] = jnp.where(at < len_ref[row], scores[-1], NEG)
    new = new_ref[row]
    new_scores = dot_nt(q, new)
    step = lax.broadcasted_iota(jnp.int32, new_scores.shape, 0) // heads
    token = lax.broadcasted_iota(jnp.int32, new_scores.shape, 1)
    new_scores = jnp.where(token <= step, new_scores, NEG)
    m = jnp.max(new_scores, axis=1, keepdims=True)
    for s in scores:
        m = jnp.maximum(m, jnp.max(s, axis=1, keepdims=True))
    new_weights = jnp.exp2((new_scores - m) * SCALE2)
    l = jnp.sum(new_weights, axis=1, keepdims=True)
    new_probs = new_weights.astype(jnp.bfloat16).astype(jnp.float32)
    new_values = new[:, :LATENT].astype(jnp.float32)
    acc = new_probs[:, 0:1] * new_values[0:1]
    for t in range(1, new.shape[0]):
        acc += new_probs[:, t : t + 1] * new_values[t : t + 1]
    for s, k in zip(scores, keys):
        p = jnp.exp2((s - m) * SCALE2)
        l += jnp.sum(p, axis=1, keepdims=True)
        acc += dot_nt(p.astype(jnp.bfloat16), k[:LATENT])
    m_ref[...] = jnp.broadcast_to(m, m_ref.shape)
    l_ref[...] = jnp.broadcast_to(l, l_ref.shape)
    acc_ref[...] = acc


def near_attention(suffix_len, queries, suffix_t, new_latent, keys):
    rows, steps, heads, width = queries.shape
    per = steps * heads
    whole = pl.BlockSpec(memory_space=pltpu.VMEM)
    return pl.pallas_call(
        near_kernel,
        grid=(rows,),
        in_specs=[
            pl.BlockSpec(memory_space=pltpu.SMEM),
            pl.BlockSpec((1, steps, heads, width), lambda r: (r, 0, 0, 0)),
            pl.BlockSpec((1,) + suffix_t.shape[1:], lambda r: (r, 0, 0)),
            whole,
        ]
        + [whole] * len(keys),
        out_specs=[
            pl.BlockSpec((per, 128), lambda r: (r, 0)),
            pl.BlockSpec((per, 128), lambda r: (r, 0)),
            pl.BlockSpec((per, LATENT), lambda r: (r, 0)),
        ],
        out_shape=[
            jax.ShapeDtypeStruct((rows * per, 128), jnp.float32),
            jax.ShapeDtypeStruct((rows * per, 128), jnp.float32),
            jax.ShapeDtypeStruct((rows * per, LATENT), jnp.float32),
        ],
        compiler_params=pltpu.CompilerParams(vmem_limit_bytes=20 * MIB),
        cost_estimate=pl.CostEstimate(
            flops=2 * rows * per * 1100 * 768, bytes_accessed=8 * MIB, transcendentals=rows * per * 768
        ),
        name="near_attention",
    )(suffix_len, queries, suffix_t, new_latent, *keys)


def far_kernel(n_keys, axis_size, pairs, q_ref, m_ref, l_ref, acc_ref, *refs):
    key_refs, out_refs, done = refs[:n_keys], refs[n_keys:-1], refs[-1]
    at = pl.program_id(0)
    per = m_ref.shape[0]
    heads, width = q_ref.shape[2:]
    q = q_ref[...].reshape(per, width)
    keys = [k[...] for k in key_refs]
    scores = [dot_nn(q, k) for k in keys]
    old_m = m_ref[:, 0:1]
    m = old_m
    for s in scores:
        m = jnp.maximum(m, jnp.max(s, axis=1, keepdims=True))
    shrink = jnp.exp2((old_m - m) * SCALE2)
    l = l_ref[:, 0:1] * shrink
    acc = acc_ref[...] * shrink
    for s, k in zip(scores, keys):
        p = jnp.exp2((s - m) * SCALE2)
        l += jnp.sum(p, axis=1, keepdims=True)
        acc += dot_nt(p.astype(jnp.bfloat16), k[:LATENT])
    attended = acc / l
    for g in range(LATENT // 128):
        done[g, pl.ds(pl.multiple_of(at * per, per), per), :] = attended[:, g * 128 : (g + 1) * 128]

    @pl.when(at == pl.num_programs(0) - 1)
    def _():
        me = lax.axis_index("roll")
        share = heads // axis_size
        for c in range(share // CHUNK_HEADS):
            for k in range(axis_size):
                first = jnp.bitwise_xor(me, k) * share + c * CHUNK_HEADS
                for i in range(CHUNK_HEADS):
                    for g in range(LATENT // 128):
                        out_refs[c * axis_size + k][
                            i * pairs : (i + 1) * pairs, g * 128 : (g + 1) * 128
                        ] = done[g, pl.ds(first + i, pairs, stride=heads), :].astype(jnp.bfloat16)


def far_attention(queries, state, keys, axis_size):
    rows, steps, heads, width = queries.shape
    pairs = rows * steps
    block_rows = 2
    per = block_rows * steps * heads
    chunks = heads // axis_size // CHUNK_HEADS
    whole = pl.BlockSpec(memory_space=pltpu.VMEM)
    return pl.pallas_call(
        functools.partial(far_kernel, len(keys), axis_size, pairs),
        grid=(rows // block_rows,),
        in_specs=[
            pl.BlockSpec((block_rows, steps, heads, width), lambda r: (r, 0, 0, 0)),
            pl.BlockSpec((per, 128), lambda r: (r, 0)),
            pl.BlockSpec((per, 128), lambda r: (r, 0)),
            pl.BlockSpec((per, LATENT), lambda r: (r, 0)),
        ]
        + [whole] * len(keys),
        out_specs=[whole] * (chunks * axis_size),
        out_shape=[
            jax.ShapeDtypeStruct((CHUNK_HEADS * pairs, LATENT), jnp.bfloat16)
        ]
        * (chunks * axis_size),
        scratch_shapes=[pltpu.VMEM((LATENT // 128, (pairs + 1) * heads, 128), jnp.float32)],
        compiler_params=pltpu.CompilerParams(vmem_limit_bytes=24 * MIB),
        cost_estimate=pl.CostEstimate(
            flops=2 * pairs * heads * 1100 * 512, bytes_accessed=8 * MIB, transcendentals=pairs * heads * 512
        ),
        name="far_attention",
    )(queries, *state, *keys)


def project_kernel(chunk, first_col, n_pieces, has_acc, last, block, *refs):
    piece_refs, refs = refs[:n_pieces], refs[n_pieces:]
    if has_acc:
        acc_ref, refs = refs[0], refs[1:]
    uv_ref, w_ref = refs[:2]
    if last:
        keep_ref, send_ref = refs[2:4]
    else:
        out_ref = refs[2]
    uv_buf, w_buf, uv_sem, w_sem = refs[-4:]
    depth, cols = w_buf.shape
    heads = uv_buf.shape[0]
    pairs = piece_refs[0].shape[0] // heads
    uv_copy = pltpu.make_async_copy(uv_ref.at[pl.ds(chunk * heads, heads)], uv_buf, uv_sem)
    uv_copy.start()
    copies = []
    for b in range(cols // block):
        here = pl.ds(b * block, block)
        copies.append(
            pltpu.make_async_copy(
                w_ref.at[pl.ds(chunk * depth, depth), pl.ds(first_col + b * block, block)],
                w_buf.at[:, here],
                w_sem.at[b],
            )
        )
        copies[-1].start()
    uv_copy.wait()
    head_out = []
    for i in range(heads):
        rows = jnp.concatenate([p[i * pairs : (i + 1) * pairs, :] for p in piece_refs], axis=0)
        head_out.append(dot_nn(rows, uv_buf[i]).astype(jnp.bfloat16))
    head_out = jnp.concatenate(head_out, axis=1)
    for b, copy in enumerate(copies):
        here = slice(b * block, (b + 1) * block)
        copy.wait()
        total = dot_nn(head_out, w_buf[:, here])
        if has_acc:
            total += acc_ref[:, here]
        if last:
            for k in range(n_pieces):
                to = send_ref if k % 2 else keep_ref
                to[k // 2 * pairs : (k // 2 + 1) * pairs, here] = total[
                    k * pairs : (k + 1) * pairs
                ].astype(jnp.bfloat16)
        else:
            out_ref[:, here] = total


def project(chunk, pieces, acc, w_uv, w_out, last, first_col, cols):
    head_v = w_uv.shape[2]
    depth = CHUNK_HEADS * head_v
    total_rows = sum(p.shape[0] for p in pieces) // CHUNK_HEADS
    block = next(b for b in (1024, 896, 512, 128) if cols % b == 0)
    vmem, hbm = pl.BlockSpec(memory_space=pltpu.VMEM), pl.BlockSpec(memory_space=pl.ANY)
    has_acc = acc is not None
    operands = list(pieces) + ([acc] if has_acc else []) + [w_uv, w_out]
    if last:
        out_shape = [jax.ShapeDtypeStruct((total_rows // 2, cols), jnp.bfloat16)] * 2
    else:
        out_shape = [jax.ShapeDtypeStruct((total_rows, cols), jnp.float32)]
    acc_spec = [vmem]
    if has_acc and acc.shape[1] != cols:
        part = first_col // cols
        acc_spec = [pl.BlockSpec((total_rows, cols), lambda i: (0, part))]
    out = pl.pallas_call(
        functools.partial(project_kernel, chunk, first_col, len(pieces), has_acc, last, block),
        grid=(1,),
        in_specs=[vmem] * len(pieces) + (acc_spec if has_acc else []) + [hbm, hbm],
        out_specs=[vmem] * len(out_shape),
        out_shape=out_shape,
        scratch_shapes=[
            pltpu.VMEM((CHUNK_HEADS,) + w_uv.shape[1:], jnp.bfloat16),
            pltpu.VMEM((depth, cols), jnp.bfloat16),
            pltpu.SemaphoreType.DMA,
            pltpu.SemaphoreType.DMA((cols // block,)),
        ],
        compiler_params=pltpu.CompilerParams(vmem_limit_bytes=32 * MIB),
        cost_estimate=pl.CostEstimate(
            flops=2 * total_rows * depth * cols, bytes_accessed=2 * depth * cols, transcendentals=0
        ),
        input_output_aliases={len(pieces): 0} if has_acc and not last else {},
        name="project",
    )(*operands)
    return out if last else out[0]


def on_device(prefix_latent, suffix_latent, suffix_len, new_latent, queries, w_uv, w_out):
    n = lax.axis_size("roll")
    rows, steps, heads, _ = queries.shape
    pairs = rows * steps
    width = w_out.shape[1]

    def swap(x, k):
        return lax.ppermute(x, "roll", [(i, i ^ k) for i in range(n)])

    own = prefix_latent.T.astype(jnp.bfloat16)
    across = [swap(own, k) for k in range(2, n, 2)]
    beside = swap(own, 1)
    forwarded = [swap(x, 1) for x in across]
    state = near_attention(
        suffix_len, queries, jnp.swapaxes(suffix_latent, 1, 2), new_latent, [own, beside]
    )
    pieces = far_attention(queries, state, across + forwarded, n)
    chunks = len(pieces) // n
    order = list(range(2, n)) + [1]
    acc = None
    for c in range(chunks):
        mine = pieces[c * n : (c + 1) * n]
        got = [mine[0]] + [None] * (n - 1)
        for k in order:
            got[k] = swap(mine[k], k)
        if c < chunks - 1:
            acc = project(c, got, acc, w_uv, w_out, False, 0, width)
    cols = width // OUT_PARTS
    outs = []
    for part in range(OUT_PARTS):
        keep, send = project(
            chunks - 1, got, acc, w_uv, w_out, True, part * cols, cols
        )
        recv = swap(send, 1)
        total = keep.astype(jnp.float32) + recv.astype(jnp.float32)
        result = total[:pairs]
        for k in range(2, n, 2):
            piece = total[k // 2 * pairs : (k // 2 + 1) * pairs].astype(jnp.bfloat16)
            result = result + swap(piece, k).astype(jnp.float32)
        outs.append(result.astype(jnp.bfloat16))
    return jnp.concatenate(outs, axis=1).reshape(rows, steps, width)


def solution(mesh):
    in_specs = (
        P(("group", "roll"), None),
        P(("group", "roll"), None, None),
        P(("group", "roll")),
        P(("group", "roll"), None, None),
        P(("group", "roll"), None, None, None),
        P("roll", None, None),
        P("roll", None),
    )
    out_specs = P(("group", "roll"), None, None)
    return jax.shard_map(
        on_device, mesh=mesh, in_specs=in_specs, out_specs=out_specs, check_vma=False
    )
```

```python
import functools
import math

import jax
import jax.numpy as jnp
from jax import lax
from jax.experimental import pallas as pl
from jax.experimental.pallas import tpu as pltpu
from jax.sharding import PartitionSpec as P

LATENT = 512
QK_HEAD = 192
SCALE2 = QK_HEAD**-0.5 * math.log2(math.e)
NEG = -1e30
CHUNK_HEADS = 4
OUT_PARTS = 2
BLOCK = 256
MIB = 2**20
NEAR_VMEM = 12 * MIB


def dot_nt(a, b):
    return lax.dot_general(a, b, (((1,), (1,)), ((), ())), preferred_element_type=jnp.float32)


def dot_nn(a, b):
    return jnp.dot(a, b, preferred_element_type=jnp.float32)


def update(scores, m, l, acc, probs_into):
    new_m = m
    for s in scores:
        new_m = jnp.maximum(new_m, jnp.max(s, axis=1, keepdims=True))
    shrink = jnp.exp2((m - new_m) * SCALE2)
    weights = [jnp.exp2((s - new_m) * SCALE2) for s in scores]
    l = l * shrink
    for p in weights:
        l += jnp.sum(p, axis=1, keepdims=True)
    return new_m, l, probs_into(acc * shrink, [p.astype(jnp.bfloat16) for p in weights])


def in_turn(tasks, score, finish):
    before = None
    for task in tasks:
        now = score(task)
        if before is not None:
            finish(*before)
        before = (task, now)
    finish(*before)


def near_call(suffix_len, queries, suffix_t, new_latent, own, beside, w_out, ahead, unit_rows, units, axis_size):
    rows, steps, heads, width = queries.shape
    tile = heads // units
    share = heads // axis_size
    per = steps * heads
    small = (queries, suffix_len, new_latent)

    def kernel(len_ref, q_ref, suf_ref, new_ref, own_ref, beside_ref, w_ref, *refs):
        w_ahead, (qs_ref, m_ref, l_ref, acc_ref) = refs[:ahead], refs[ahead : ahead + 4]
        q_buf, len_buf, new_buf, suf_buf, sems, suf_sems, w_sems = refs[ahead + 4 :]
        pairs = [(q_ref, q_buf), (len_ref, len_buf), (new_ref, new_buf)]
        copies = [pltpu.make_async_copy(x, y, sems.at[i]) for i, (x, y) in enumerate(pairs)]
        suf_copies = [
            pltpu.make_async_copy(suf_ref.at[r], suf_buf.at[r], suf_sems.at[r]) for r in range(rows)
        ]
        w_copies = [
            pltpu.make_async_copy(w_ref.at[pl.ds(i * unit_rows, unit_rows)], to, w_sems.at[i])
            for i, to in enumerate(w_ahead)
        ]
        for copy in copies + suf_copies + w_copies:
            copy.start()
        for copy in copies:
            copy.wait()
        keys = [own_ref[...], beside_ref[...]]

        def sort(r):
            by_unit = [[] for _ in range(units)]
            for s in range(steps):
                q = q_buf[r, s].astype(jnp.float32)
                for u in range(units):
                    picked = [
                        q[j * share + u * CHUNK_HEADS : j * share + (u + 1) * CHUNK_HEADS]
                        for j in range(axis_size)
                    ]
                    by_unit[u].append(jnp.concatenate(picked, axis=0).astype(jnp.bfloat16))
            for u in range(units):
                for s in range(steps):
                    qs_ref[u, r * steps + s] = by_unit[u][s]
            return jnp.concatenate([x for unit in by_unit for x in unit], axis=0)

        def score(first):
            q = [sort(first + i) for i in range(BLOCK // per)]
            both = jnp.concatenate(q, axis=0)
            scores = [dot_nn(both, k) for k in keys]
            old, new = [], []
            for i, x in enumerate(q):
                suf_copies[first + i].wait()
                s = dot_nn(x, suf_buf[first + i])
                at = lax.broadcasted_iota(jnp.int32, s.shape, 1)
                old.append(jnp.where(at < len_buf[first + i], s, NEG))
                s = dot_nt(x, new_buf[first + i])
                step = lax.broadcasted_iota(jnp.int32, s.shape, 0) // tile % steps
                token = lax.broadcasted_iota(jnp.int32, s.shape, 1)
                new.append(jnp.where(token <= step, s, NEG))
            return scores + [jnp.concatenate(x, axis=0) for x in (old, new)]

        def finish(first, scores):
            m = functools.reduce(
                jnp.maximum, [jnp.max(s, axis=1, keepdims=True) for s in scores]
            )
            weights = [jnp.exp2((s - m) * SCALE2) for s in scores]
            l = sum(jnp.sum(p, axis=1, keepdims=True) for p in weights)
            probs = [p.astype(jnp.bfloat16) for p in weights]
            acc = dot_nt(probs[0], keys[0][:LATENT]) + dot_nt(probs[1], keys[1][:LATENT])
            new_probs = probs[3].astype(jnp.float32)
            for i in range(BLOCK // per):
                here = slice(i * per, (i + 1) * per)
                part = acc[here] + dot_nt(probs[2][here], suf_buf[first + i, :LATENT])
                values = new_buf[first + i][:, :LATENT].astype(jnp.float32)
                for t in range(steps):
                    part += new_probs[here, t : t + 1] * values[t : t + 1]
                there = slice((first + i) * steps, (first + i + 1) * steps)
                lead = (units, steps, tile)
                m_ref[:, there] = jnp.broadcast_to(m[here], (per, 128)).reshape(lead + (128,))
                l_ref[:, there] = jnp.broadcast_to(l[here], (per, 128)).reshape(lead + (128,))
                acc_ref[:, there] = part.reshape(lead + (LATENT,))

        in_turn(range(0, rows, BLOCK // per), score, finish)
        for copy in w_copies:
            copy.wait()

    vmem, hbm = pl.BlockSpec(memory_space=pltpu.VMEM), pl.BlockSpec(memory_space=pltpu.HBM)
    lead = (units, rows * steps, tile)
    f32 = jnp.float32
    return pl.pallas_call(
        kernel,
        in_specs=[hbm, hbm, hbm, hbm, vmem, vmem, hbm],
        out_specs=[vmem] * (ahead + 4),
        out_shape=[pltpu.VMEM((unit_rows, w_out.shape[1]), w_out.dtype)] * ahead
        + [
            jax.ShapeDtypeStruct(lead + (width,), queries.dtype),
            jax.ShapeDtypeStruct(lead + (128,), f32),
            jax.ShapeDtypeStruct(lead + (128,), f32),
            jax.ShapeDtypeStruct(lead + (LATENT,), f32),
        ],
        scratch_shapes=[
            pltpu.VMEM(queries.shape, queries.dtype),
            pltpu.SMEM(suffix_len.shape, jnp.int32),
            pltpu.VMEM(new_latent.shape, jnp.bfloat16),
            pltpu.VMEM(suffix_t.shape, jnp.bfloat16),
            pltpu.SemaphoreType.DMA((len(small),)),
            pltpu.SemaphoreType.DMA((rows,)),
            pltpu.SemaphoreType.DMA((ahead,)),
        ],
        compiler_params=pltpu.CompilerParams(vmem_limit_bytes=NEAR_VMEM),
        cost_estimate=pl.CostEstimate(
            flops=4 * rows * per * 1100 * 768,
            bytes_accessed=4 * MIB + 2 * ahead * unit_rows * w_out.shape[1],
            transcendentals=rows * per * 768,
        ),
        name="near_attention",
    )(suffix_len, queries, suffix_t, new_latent, own, beside, w_out)


def merge(units, keys, q_ref, m_ref, l_ref, acc_ref, store):
    _, pairs, tile, width = q_ref.shape
    step = BLOCK // tile
    tasks = [(u, slice(first, first + step)) for u in units for first in range(0, pairs, step)]

    def score(here):
        q = q_ref[here].reshape(BLOCK, width)
        return [dot_nn(q, k) for k in keys]

    def finish(here, scores):
        store(
            here,
            *update(
                scores,
                m_ref[here].reshape(BLOCK, 128)[:, 0:1],
                l_ref[here].reshape(BLOCK, 128)[:, 0:1],
                acc_ref[here].reshape(BLOCK, LATENT),
                lambda acc, ps: acc + sum(dot_nt(p, k[:LATENT]) for p, k in zip(ps, keys)),
            ),
        )

    in_turn(tasks, score, finish)


def middle_call(queries, state, keys):
    units, pairs, tile, _ = queries.shape

    def kernel(q_ref, m_ref, l_ref, acc_ref, *refs):
        key_refs, (m_out, l_out, acc_out) = refs[: len(keys)], refs[len(keys) :]

        def store(here, m, l, acc):
            lead = (BLOCK // tile, tile)
            m_out[here] = jnp.broadcast_to(m, (BLOCK, 128)).reshape(lead + (128,))
            l_out[here] = jnp.broadcast_to(l, (BLOCK, 128)).reshape(lead + (128,))
            acc_out[here] = acc.reshape(lead + (LATENT,))

        merge(range(units), [k[...] for k in key_refs], q_ref, m_ref, l_ref, acc_ref, store)

    vmem = pl.BlockSpec(memory_space=pltpu.VMEM)
    return pl.pallas_call(
        kernel,
        in_specs=[vmem] * (4 + len(keys)),
        out_specs=[vmem] * 3,
        out_shape=[jax.ShapeDtypeStruct(x.shape, x.dtype) for x in state],
        compiler_params=pltpu.CompilerParams(vmem_limit_bytes=10 * MIB),
        cost_estimate=pl.CostEstimate(
            flops=2 * units * pairs * tile * 1100 * 256 * len(keys),
            bytes_accessed=4 * MIB,
            transcendentals=0,
        ),
        name="middle_attention",
    )(queries, *state, *keys)


def far_call(first, size, queries, state, keys, axis_size):
    _, pairs, tile, _ = queries.shape
    per_unit = pairs * tile

    def kernel(q_ref, m_ref, l_ref, acc_ref, *refs):
        key_refs, out_refs, done = refs[: len(keys)], refs[len(keys) : -1], refs[-1]

        def store(here, m, l, acc):
            attended = acc / l
            at = (here[0] - first) * per_unit + here[1].start * tile
            for g in range(LATENT // 128):
                done[g, at : at + BLOCK, :] = attended[:, g * 128 : (g + 1) * 128]

        keys_now = [k[...] for k in key_refs]
        merge(range(first, first + size), keys_now, q_ref, m_ref, l_ref, acc_ref, store)
        me = lax.axis_index("roll")
        for k in range(axis_size):
            there = jnp.bitwise_xor(me, k) * CHUNK_HEADS
            for u in range(size):
                for i in range(CHUNK_HEADS):
                    at = (u * CHUNK_HEADS + i) * pairs
                    for g in range(LATENT // 128):
                        out_refs[k][at : at + pairs, g * 128 : (g + 1) * 128] = done[
                            g, pl.ds(u * per_unit + there + i, pairs, stride=tile), :
                        ].astype(jnp.bfloat16)

    vmem = pl.BlockSpec(memory_space=pltpu.VMEM)
    return pl.pallas_call(
        kernel,
        in_specs=[vmem] * (4 + len(keys)),
        out_specs=[vmem] * axis_size,
        out_shape=[jax.ShapeDtypeStruct((size * CHUNK_HEADS * pairs, LATENT), jnp.bfloat16)]
        * axis_size,
        scratch_shapes=[pltpu.VMEM((LATENT // 128, size * per_unit + tile, 128), jnp.float32)],
        compiler_params=pltpu.CompilerParams(vmem_limit_bytes=10 * MIB),
        cost_estimate=pl.CostEstimate(
            flops=2 * size * per_unit * 1100 * 256 * len(keys), bytes_accessed=MIB, transcendentals=0
        ),
        name="far_attention",
    )(queries, *state, *keys)


def project(first_head, heads, pieces, acc, w_uv, w_units, kept=None, first_col=0, cols=None, bring=(None, ())):
    n_pieces = len(pieces)
    pairs = pieces[0].shape[0] // heads
    total_rows = n_pieces * pairs
    unit_rows, width = w_units[0].shape
    cols = width if cols is None else cols
    block = next(b for b in (1792, 1024, 896, 512, 128) if cols % b == 0)
    w_all, missing = bring

    def kernel(*refs):
        refs = list(refs)
        piece_refs = [refs.pop(0) for _ in pieces]
        acc_ref = refs.pop(0) if acc is not None else None
        uv_ref = refs.pop(0)
        w_refs = [refs.pop(0) for _ in w_units]
        copies = []
        if missing:
            all_ref, sem = refs.pop(0), refs[-1]
            for i, u in enumerate(missing):
                rows = pl.ds(u * unit_rows, unit_rows)
                copies.append(pltpu.make_async_copy(all_ref.at[rows], refs[1 + i], sem.at[i]))
                copies[-1].start()
        head_out = []
        for i in range(heads):
            rows = jnp.concatenate([p[i * pairs : (i + 1) * pairs, :] for p in piece_refs], axis=0)
            head_out.append(dot_nn(rows, uv_ref[first_head + i]).astype(jnp.bfloat16))
        head_out = jnp.concatenate(head_out, axis=1)
        for b in range(cols // block):
            here = slice(b * block, (b + 1) * block)
            there = slice(first_col + b * block, first_col + (b + 1) * block)
            total = sum(
                dot_nn(head_out[:, u * unit_rows : (u + 1) * unit_rows], w_ref[:, there])
                for u, w_ref in enumerate(w_refs)
            )
            if acc_ref is not None:
                total += acc_ref[:, there]
            if kept is None:
                refs[0][:, here] = total
                continue
            at = [0, 0]
            for k in range(n_pieces):
                side = 0 if k in kept else 1
                refs[side][at[side] * pairs : (at[side] + 1) * pairs, here] = total[
                    k * pairs : (k + 1) * pairs
                ].astype(jnp.bfloat16)
                at[side] += 1
        for copy in copies:
            copy.wait()

    vmem, hbm = pl.BlockSpec(memory_space=pltpu.VMEM), pl.BlockSpec(memory_space=pltpu.HBM)
    operands = list(pieces) + ([acc] if acc is not None else []) + [w_uv, *w_units]
    in_specs = [vmem] * len(operands)
    scratch = []
    if kept is not None:
        out_shape = [jax.ShapeDtypeStruct((total_rows // 2, cols), jnp.bfloat16)] * 2
    else:
        out_shape = [jax.ShapeDtypeStruct((total_rows, cols), jnp.float32)]
    if missing:
        operands.append(w_all)
        in_specs.append(hbm)
        out_shape += [pltpu.VMEM(w_units[0].shape, w_all.dtype)] * len(missing)
        scratch = [pltpu.SemaphoreType.DMA((len(missing),))]
    depth = heads * w_uv.shape[2]
    return pl.pallas_call(
        kernel,
        in_specs=in_specs,
        out_specs=[vmem] * len(out_shape),
        out_shape=out_shape,
        scratch_shapes=scratch,
        compiler_params=pltpu.CompilerParams(vmem_limit_bytes=8 * MIB),
        cost_estimate=pl.CostEstimate(
            flops=8 * total_rows * depth * cols, bytes_accessed=2 * depth * cols, transcendentals=0
        ),
        input_output_aliases={n_pieces: 0} if acc is not None and kept is None else {},
        name="project",
    )(*operands)


def last_sums(rows, steps, width, parts):
    pairs = rows * steps
    flat = [x for part in parts for x in part]
    cols = width // len(parts)

    def kernel(*refs):
        refs, out_ref = list(refs[:-1]), refs[-1]
        for i, part in enumerate(parts):
            total = None
            for _, first in part:
                x = refs.pop(0)[first : first + pairs, :].astype(jnp.float32)
                total = x if total is None else total + x
            out_ref[:, :, i * cols : (i + 1) * cols] = total.astype(jnp.bfloat16).reshape(
                rows, steps, cols
            )

    vmem = pl.BlockSpec(memory_space=pltpu.VMEM)
    return pl.pallas_call(
        kernel,
        in_specs=[vmem] * len(flat),
        out_specs=vmem,
        out_shape=jax.ShapeDtypeStruct((rows, steps, width), jnp.bfloat16),
        compiler_params=pltpu.CompilerParams(vmem_limit_bytes=8 * MIB),
        name="last_sums",
    )(*[x for x, _ in flat])


def on_device(prefix_latent, suffix_latent, suffix_len, new_latent, queries, w_uv, w_out):
    n = lax.axis_size("roll")
    rows, steps, heads, _ = queries.shape
    pairs = rows * steps
    width = w_out.shape[1]
    share = heads // n
    units = share // CHUNK_HEADS
    unit_rows = CHUNK_HEADS * w_uv.shape[2]
    chunks = [(0, 1), (1, units - 2), (units - 1, 1)] if units > 2 else [(u, 1) for u in range(units)]
    ahead = max(1, units // 2)

    def swap(x, k):
        return lax.ppermute(x, "roll", [(i, i ^ k) for i in range(n)])

    own = prefix_latent.T.astype(jnp.bfloat16)
    across = [swap(own, k) for k in range(2, n, 2)]
    beside = swap(own, 1)
    *w_units, queries, m, l, acc = near_call(
        suffix_len,
        queries,
        jnp.swapaxes(suffix_latent, 1, 2),
        new_latent,
        own,
        beside,
        w_out,
        ahead,
        unit_rows,
        units,
        n,
    )
    *across, m = lax.optimization_barrier((*across, m))
    forwarded = [swap(x, 1) for x in across]
    state = middle_call(queries, (m, l, acc), across)
    got = []
    for first, size in chunks:
        mine = far_call(first, size, queries, state, forwarded, n)
        there = [mine[0]] + [None] * (n - 1)
        for k in list(range(2, n)) + [1]:
            there[k] = swap(mine[k], k)
        got.append(there)
    acc = None
    for c, (first, size) in enumerate(chunks[:-1]):
        missing = range(len(w_units), units) if c == 0 else ()
        acc, *brought = project(
            first * CHUNK_HEADS,
            size * CHUNK_HEADS,
            got[c],
            acc,
            w_uv,
            w_units[first : first + size],
            bring=(w_out, missing),
        )
        w_units += brought
    first, size = chunks[-1]
    cols = width // OUT_PARTS
    parts = []
    for part in range(OUT_PARTS):
        odd = part % 2
        kept = tuple(k for k in range(n) if k == 0 or (k != 1 and k % 2 == odd))
        keep, send = project(
            first * CHUNK_HEADS,
            size * CHUNK_HEADS,
            got[-1],
            acc,
            w_uv,
            w_units[first : first + size],
            kept=kept,
            first_col=part * cols,
            cols=cols,
        )
        left = [k for k in range(n) if k not in kept]
        recv = swap(send, 1)

        def piece(x, i):
            return x[i * pairs : (i + 1) * pairs].astype(jnp.float32)

        terms = [(keep, 0), (recv, left.index(1) * pairs)]
        for i, k in enumerate(kept[1:]):
            both = piece(keep, i + 1) + piece(recv, left.index(k ^ 1))
            terms.append((swap(both.astype(jnp.bfloat16), k), 0))
        parts.append(terms)
    return last_sums(rows, steps, width, parts)


def solution(mesh):
    in_specs = (
        P(("group", "roll"), None),
        P(("group", "roll"), None, None),
        P(("group", "roll")),
        P(("group", "roll"), None, None),
        P(("group", "roll"), None, None, None),
        P("roll", None, None),
        P("roll", None),
    )
    out_specs = P(("group", "roll"), None, None)
    return jax.shard_map(
        on_device, mesh=mesh, in_specs=in_specs, out_specs=out_specs, check_vma=False
    )
```

```python
import functools
import math

import jax
import jax.numpy as jnp
from jax import lax
from jax.experimental import pallas as pl
from jax.experimental.pallas import tpu as pltpu
from jax.sharding import PartitionSpec as P

LATENT = 512
QK_HEAD = 192
SCALE2 = QK_HEAD**-0.5 * math.log2(math.e)
NEG = -1e30
CHUNK_HEADS = 4
OUT_PARTS = 2
BLOCK = 256
MIB = 2**20
W_PIECES = 2
PAUSE_FLOPS = 10**10
PAUSE_BYTES = 30 * MIB


def dot_nt(a, b):
    return lax.dot_general(a, b, (((1,), (1,)), ((), ())), preferred_element_type=jnp.float32)


def dot_nn(a, b):
    return jnp.dot(a, b, preferred_element_type=jnp.float32)


def pause():
    def kernel(out_ref):
        out_ref[...] = jnp.zeros_like(out_ref)

    return pl.pallas_call(
        kernel,
        out_specs=pl.BlockSpec(memory_space=pltpu.VMEM),
        out_shape=pltpu.VMEM((8, 128), jnp.float32),
        cost_estimate=pl.CostEstimate(
            flops=PAUSE_FLOPS, bytes_accessed=PAUSE_BYTES, transcendentals=0
        ),
        name="pause",
    )()


def call(body, operands, in_specs, out_shape, scratch, bring, limit, flops, name, aliases=None):
    w_out, piece_rows, pieces = bring
    vmem, hbm = pl.BlockSpec(memory_space=pltpu.VMEM), pl.BlockSpec(memory_space=pltpu.HBM)
    n_in, n_out = len(operands), len(out_shape)
    copied = 0
    if pieces:
        operands, in_specs = [*operands, w_out], [*in_specs, hbm]
        out_shape = [*out_shape] + [pltpu.VMEM((piece_rows, w_out.shape[1]), w_out.dtype)] * len(pieces)
        scratch = [*scratch, pltpu.SemaphoreType.DMA((len(pieces),))]
        copied = 2 * len(pieces) * piece_rows * w_out.shape[1]

    def kernel(*refs):
        ins, rest = refs[: len(operands)], refs[len(operands) :]
        outs, rest = rest[: len(out_shape)], rest[len(out_shape) :]
        copies = []
        for i, piece in enumerate(pieces):
            rows = pl.ds(piece * piece_rows, piece_rows)
            copies.append(pltpu.make_async_copy(ins[-1].at[rows], outs[n_out + i], rest[-1].at[i]))
        for copy in copies:
            copy.start()
        body(ins[:n_in], outs[:n_out], rest[: len(scratch) - bool(pieces)])
        for copy in copies:
            copy.wait()

    out = pl.pallas_call(
        kernel,
        in_specs=in_specs,
        out_specs=[vmem] * len(out_shape),
        out_shape=out_shape,
        scratch_shapes=scratch,
        compiler_params=pltpu.CompilerParams(vmem_limit_bytes=limit * MIB),
        cost_estimate=pl.CostEstimate(
            flops=flops, bytes_accessed=4 * MIB + copied, transcendentals=0
        ),
        input_output_aliases=aliases or {},
        name=name,
    )(*operands)
    return out[:n_out], list(out[n_out:])


def update(scores, m, l, acc, probs_into):
    new_m = m
    for s in scores:
        new_m = jnp.maximum(new_m, jnp.max(s, axis=1, keepdims=True))
    shrink = jnp.exp2((m - new_m) * SCALE2)
    weights = [jnp.exp2((s - new_m) * SCALE2) for s in scores]
    l = l * shrink
    for p in weights:
        l += jnp.sum(p, axis=1, keepdims=True)
    return new_m, l, probs_into(acc * shrink, [p.astype(jnp.bfloat16) for p in weights])


def in_turn(tasks, score, finish):
    def some(first, count):
        before = None
        for i in range(count):
            task = first + i
            now = score(task)
            if before is not None:
                finish(*before)
            before = (task, now)
        finish(*before)

    if tasks % 2 or tasks < 4:
        some(0, tasks)
    else:

        @pl.loop(0, 2)
        def _(i):
            some(i * (tasks // 2), tasks // 2)


def near_call(paused, suffix_len, queries, suffix_t, new_latent, own, beside, units, axis_size, bring):
    rows, steps, heads, width = queries.shape
    tile = heads // units
    share = heads // axis_size
    per = steps * heads

    def body(ins, outs, _):
        _, len_buf, q_buf, suf_buf, new_buf, own_ref, beside_ref = ins
        qs_ref, m_ref, l_ref, acc_ref = outs
        keys = [own_ref[...], beside_ref[...]]

        def sort(r):
            by_unit = [[] for _ in range(units)]
            for s in range(steps):
                q = q_buf[r, s].astype(jnp.float32)
                for u in range(units):
                    picked = [
                        q[j * share + u * CHUNK_HEADS : j * share + (u + 1) * CHUNK_HEADS]
                        for j in range(axis_size)
                    ]
                    by_unit[u].append(jnp.concatenate(picked, axis=0).astype(jnp.bfloat16))
            for u in range(units):
                for s in range(steps):
                    qs_ref[u, r * steps + s] = by_unit[u][s]
            return jnp.concatenate([x for unit in by_unit for x in unit], axis=0)

        def score(task):
            first = task * (BLOCK // per)
            q = [sort(first + i) for i in range(BLOCK // per)]
            both = jnp.concatenate(q, axis=0)
            scores = [dot_nn(both, k) for k in keys]
            old, new = [], []
            for i, x in enumerate(q):
                s = dot_nn(x, suf_buf[first + i])
                at = lax.broadcasted_iota(jnp.int32, s.shape, 1)
                old.append(jnp.where(at < len_buf[first + i], s, NEG))
                s = dot_nt(x, new_buf[first + i])
                step = lax.broadcasted_iota(jnp.int32, s.shape, 0) // tile % steps
                token = lax.broadcasted_iota(jnp.int32, s.shape, 1)
                new.append(jnp.where(token <= step, s, NEG))
            return scores + [jnp.concatenate(x, axis=0) for x in (old, new)]

        def finish(task, scores):
            first = task * (BLOCK // per)
            m = functools.reduce(
                jnp.maximum, [jnp.max(s, axis=1, keepdims=True) for s in scores]
            )
            weights = [jnp.exp2((s - m) * SCALE2) for s in scores]
            l = sum(jnp.sum(p, axis=1, keepdims=True) for p in weights)
            probs = [p.astype(jnp.bfloat16) for p in weights]
            acc = dot_nt(probs[0], keys[0][:LATENT]) + dot_nt(probs[1], keys[1][:LATENT])
            new_probs = probs[3].astype(jnp.float32)
            for i in range(BLOCK // per):
                here = slice(i * per, (i + 1) * per)
                part = acc[here] + dot_nt(probs[2][here], suf_buf[first + i, :LATENT])
                values = new_buf[first + i][:, :LATENT].astype(jnp.float32)
                for t in range(steps):
                    part += new_probs[here, t : t + 1] * values[t : t + 1]
                there = pl.ds((first + i) * steps, steps)
                lead = (units, steps, tile)
                m_ref[:, there] = jnp.broadcast_to(m[here], (per, 128)).reshape(lead + (128,))
                l_ref[:, there] = jnp.broadcast_to(l[here], (per, 128)).reshape(lead + (128,))
                acc_ref[:, there] = part.reshape(lead + (LATENT,))

        in_turn(rows * per // BLOCK, score, finish)

    vmem, smem = pl.BlockSpec(memory_space=pltpu.VMEM), pl.BlockSpec(memory_space=pltpu.SMEM)
    lead = (units, rows * steps, tile)
    f32 = jnp.float32
    return call(
        body,
        [paused, suffix_len, queries, suffix_t, new_latent, own, beside],
        [vmem, smem] + [vmem] * 5,
        [
            jax.ShapeDtypeStruct(lead + (width,), queries.dtype),
            jax.ShapeDtypeStruct(lead + (128,), f32),
            jax.ShapeDtypeStruct(lead + (128,), f32),
            jax.ShapeDtypeStruct(lead + (LATENT,), f32),
        ],
        [],
        bring,
        24,
        4 * rows * per * 1100 * 768,
        "near_attention",
    )


def merge(first, size, keys, q_ref, m_ref, l_ref, acc_ref, store):
    _, pairs, tile, width = q_ref.shape
    step = BLOCK // tile
    blocks = pairs // step

    def at(task):
        return first + task // blocks, pl.ds(task % blocks * step, step)

    def score(task):
        here = at(task)
        q = q_ref[here].reshape(BLOCK, width)
        return [dot_nn(q, k) for k in keys]

    def finish(task, scores):
        here = at(task)
        store(
            task,
            here,
            *update(
                scores,
                m_ref[here].reshape(BLOCK, 128)[:, 0:1],
                l_ref[here].reshape(BLOCK, 128)[:, 0:1],
                acc_ref[here].reshape(BLOCK, LATENT),
                lambda acc, ps: acc + sum(dot_nt(p, k[:LATENT]) for p, k in zip(ps, keys)),
            ),
        )

    in_turn(size * blocks, score, finish)


def middle_call(queries, state, keys, bring):
    units, pairs, tile, _ = queries.shape

    def body(ins, outs, _):
        q_ref, m_ref, l_ref, acc_ref, *key_refs = ins
        m_out, l_out, acc_out = outs

        def store(task, here, m, l, acc):
            lead = (BLOCK // tile, tile)
            m_out[here] = jnp.broadcast_to(m, (BLOCK, 128)).reshape(lead + (128,))
            l_out[here] = jnp.broadcast_to(l, (BLOCK, 128)).reshape(lead + (128,))
            acc_out[here] = acc.reshape(lead + (LATENT,))

        merge(0, units, [k[...] for k in key_refs], q_ref, m_ref, l_ref, acc_ref, store)

    operands = [queries, *state, *keys]
    return call(
        body,
        operands,
        [pl.BlockSpec(memory_space=pltpu.VMEM)] * len(operands),
        [jax.ShapeDtypeStruct(x.shape, x.dtype) for x in state],
        [],
        bring,
        28 if bring[2] else 10,
        2 * units * pairs * tile * 1100 * 256 * len(keys),
        "middle_attention",
    )


def far_call(first, size, queries, state, keys, axis_size, bring):
    _, pairs, tile, _ = queries.shape
    per_unit = pairs * tile

    def body(ins, out_refs, scratch):
        q_ref, m_ref, l_ref, acc_ref, *key_refs = ins
        (done,) = scratch

        def store(task, here, m, l, acc):
            attended = acc / l
            rows = pl.ds(task * BLOCK, BLOCK)
            for g in range(LATENT // 128):
                done[g, rows, :] = attended[:, g * 128 : (g + 1) * 128]

        keys_now = [k[...] for k in key_refs]
        merge(first, size, keys_now, q_ref, m_ref, l_ref, acc_ref, store)
        me = lax.axis_index("roll")
        for k in range(axis_size):
            there = jnp.bitwise_xor(me, k) * CHUNK_HEADS
            for u in range(size):
                for i in range(CHUNK_HEADS):
                    at = (u * CHUNK_HEADS + i) * pairs
                    for g in range(LATENT // 128):
                        out_refs[k][at : at + pairs, g * 128 : (g + 1) * 128] = done[
                            g, pl.ds(u * per_unit + there + i, pairs, stride=tile), :
                        ].astype(jnp.bfloat16)

    operands = [queries, *state, *keys]
    return call(
        body,
        operands,
        [pl.BlockSpec(memory_space=pltpu.VMEM)] * len(operands),
        [jax.ShapeDtypeStruct((size * CHUNK_HEADS * pairs, LATENT), jnp.bfloat16)] * axis_size,
        [pltpu.VMEM((LATENT // 128, size * per_unit + tile, 128), jnp.float32)],
        bring,
        24 if bring[2] else 10,
        2 * size * per_unit * 1100 * 256 * len(keys),
        "far_attention",
    )


def project(first_head, heads, pieces, acc, w_uv, w_pieces, bring, kept=None, first_col=0, cols=None):
    pairs = pieces[0].shape[0] // heads
    total_rows = len(pieces) * pairs
    piece_rows, width = w_pieces[0].shape
    cols = width if cols is None else cols
    block = next(b for b in (1792, 1024, 896, 512, 128) if cols % b == 0)

    def body(ins, outs, _):
        ins = list(ins)
        piece_refs = [ins.pop(0) for _ in pieces]
        acc_ref = ins.pop(0) if acc is not None else None
        uv_ref, *w_refs = ins
        head_out = []
        for i in range(heads):
            rows = jnp.concatenate([p[i * pairs : (i + 1) * pairs, :] for p in piece_refs], axis=0)
            head_out.append(dot_nn(rows, uv_ref[first_head + i]).astype(jnp.bfloat16))
        head_out = jnp.concatenate(head_out, axis=1)

        def block_of(b):
            here = pl.ds(b * block, block)
            there = pl.ds(first_col + b * block, block)
            total = sum(
                dot_nn(head_out[:, i * piece_rows : (i + 1) * piece_rows], w_ref[:, there])
                for i, w_ref in enumerate(w_refs)
            )
            if acc_ref is not None:
                total += acc_ref[:, there]
            if kept is None:
                outs[0][:, here] = total
                return
            at = [0, 0]
            for k in range(len(pieces)):
                side = 0 if k in kept else 1
                outs[side][at[side] * pairs : (at[side] + 1) * pairs, here] = total[
                    k * pairs : (k + 1) * pairs
                ].astype(jnp.bfloat16)
                at[side] += 1

        if bring[2]:
            pl.loop(0, cols // block)(block_of)
        else:
            for b in range(cols // block):
                block_of(b)

    operands = [*pieces] + ([acc] if acc is not None else []) + [w_uv, *w_pieces]
    if kept is not None:
        out_shape = [jax.ShapeDtypeStruct((total_rows // 2, cols), jnp.bfloat16)] * 2
    else:
        out_shape = [jax.ShapeDtypeStruct((total_rows, cols), jnp.float32)]
    return call(
        body,
        operands,
        [pl.BlockSpec(memory_space=pltpu.VMEM)] * len(operands),
        out_shape,
        [],
        bring,
        14 if bring[2] else 8,
        8 * total_rows * heads * w_uv.shape[2] * cols,
        "project",
        {len(pieces): 0} if acc is not None and kept is None else {},
    )


def last_sums(rows, steps, width, parts):
    pairs = rows * steps
    flat = [x for part in parts for x in part]
    cols = width // len(parts)

    def kernel(*refs):
        refs, out_ref = list(refs[:-1]), refs[-1]
        for i, part in enumerate(parts):
            total = None
            for _, first in part:
                x = refs.pop(0)[first : first + pairs, :].astype(jnp.float32)
                total = x if total is None else total + x
            out_ref[:, :, i * cols : (i + 1) * cols] = total.astype(jnp.bfloat16).reshape(
                rows, steps, cols
            )

    vmem = pl.BlockSpec(memory_space=pltpu.VMEM)
    return pl.pallas_call(
        kernel,
        in_specs=[vmem] * len(flat),
        out_specs=vmem,
        out_shape=jax.ShapeDtypeStruct((rows, steps, width), jnp.bfloat16),
        compiler_params=pltpu.CompilerParams(vmem_limit_bytes=8 * MIB),
        name="last_sums",
    )(*[x for x, _ in flat])


def on_device(prefix_latent, suffix_latent, suffix_len, new_latent, queries, w_uv, w_out):
    n = lax.axis_size("roll")
    rows, steps, heads, _ = queries.shape
    pairs = rows * steps
    width = w_out.shape[1]
    share = heads // n
    units = share // CHUNK_HEADS
    chunks = [(0, 1), (1, units - 2), (units - 1, 1)] if units > 2 else [(u, 1) for u in range(units)]
    piece_rows = CHUNK_HEADS * w_uv.shape[2] // W_PIECES
    n_pieces = units * W_PIECES
    if len(chunks) == 3 and n_pieces == 8:
        brings = {
            "near": [0, 1, 2, 3],
            "middle": [4],
            ("project", 0): [5],
            ("project", 1): [6, 7],
        }
    else:
        half = n_pieces // 2
        brings = {"near": list(range(half)), "middle": list(range(half, n_pieces))}
    held = {}

    def bring(who):
        return (w_out, piece_rows, brings.get(who, []))

    def keep(who, result):
        out, brought = result
        held.update(zip(brings.get(who, []), brought))
        return out

    def swap(x, k):
        return lax.ppermute(x, "roll", [(i, i ^ k) for i in range(n)])

    own = prefix_latent.T.astype(jnp.bfloat16)
    own, paused = lax.optimization_barrier((own, pause()))
    across = [swap(own, k) for k in range(2, n, 2)]
    beside = swap(own, 1)
    queries, m, l, acc = keep(
        "near",
        near_call(
            paused,
            suffix_len,
            queries,
            jnp.swapaxes(suffix_latent, 1, 2),
            new_latent,
            own,
            beside,
            units,
            n,
            bring("near"),
        ),
    )
    *across, m = lax.optimization_barrier((*across, m))
    forwarded = [swap(x, 1) for x in across]
    state = keep("middle", middle_call(queries, (m, l, acc), across, bring("middle")))
    got = []
    for c, (first, size) in enumerate(chunks):
        if c >= 2:
            queries, *got[c - 2] = lax.optimization_barrier((queries, *got[c - 2]))
        who = ("far", c)
        mine = keep(who, far_call(first, size, queries, state, forwarded, n, bring(who)))
        if c >= 2:
            *mine, got[c - 2] = lax.optimization_barrier((*mine, got[c - 2]))
        *mine, queries = lax.optimization_barrier((*mine, queries))
        there = [mine[0]] + [None] * (n - 1)
        for k in range(1, n):
            there[k] = swap(mine[k], k)
        got.append(there)
    acc = None

    def pieces_of(first, size):
        return [held[i] for i in range(first * W_PIECES, (first + size) * W_PIECES)]

    for c, (first, size) in enumerate(chunks[:-1]):
        who = ("project", c)
        (acc,) = keep(
            who,
            project(
                first * CHUNK_HEADS,
                size * CHUNK_HEADS,
                got[c],
                acc,
                w_uv,
                pieces_of(first, size),
                bring(who),
            ),
        )
    first, size = chunks[-1]
    cols = width // OUT_PARTS
    parts = []
    for part in range(OUT_PARTS):
        odd = part % 2
        kept = tuple(k for k in range(n) if k == 0 or (k != 1 and k % 2 == odd))
        (stay, send), _ = project(
            first * CHUNK_HEADS,
            size * CHUNK_HEADS,
            got[-1],
            acc,
            w_uv,
            pieces_of(first, size),
            bring(None),
            kept,
            part * cols,
            cols,
        )
        left = [k for k in range(n) if k not in kept]
        recv = swap(send, 1)

        def piece(x, i):
            return x[i * pairs : (i + 1) * pairs].astype(jnp.float32)

        terms = [(stay, 0), (recv, left.index(1) * pairs)]
        for i, k in enumerate(kept[1:]):
            both = piece(stay, i + 1) + piece(recv, left.index(k ^ 1))
            terms.append((swap(both.astype(jnp.bfloat16), k), 0))
        parts.append(terms)
    return last_sums(rows, steps, width, parts)


def solution(mesh):
    in_specs = (
        P(("group", "roll"), None),
        P(("group", "roll"), None, None),
        P(("group", "roll")),
        P(("group", "roll"), None, None),
        P(("group", "roll"), None, None, None),
        P("roll", None, None),
        P("roll", None),
    )
    out_specs = P(("group", "roll"), None, None)
    return jax.shard_map(
        on_device, mesh=mesh, in_specs=in_specs, out_specs=out_specs, check_vma=False
    )
```

```python
import functools
import math

import jax
import jax.numpy as jnp
from jax import lax
from jax.experimental import pallas as pl
from jax.experimental.pallas import tpu as pltpu
from jax.sharding import PartitionSpec as P

LATENT = 512
QK_HEAD = 192
SCALE2 = QK_HEAD**-0.5 * math.log2(math.e)
NEG = -1e30
CHUNK_HEADS = 4
OUT_PARTS = 2
BLOCK = 256
MIB = 2**20
W_PIECES = 2
NEAR_LIMIT = 20
FAR_LIMIT = 20
PROJECT_LIMIT = 10
PAUSE_FLOPS = 10**10
PAUSE_BYTES = 30 * MIB


def dot_nt(a, b):
    return lax.dot_general(a, b, (((1,), (1,)), ((), ())), preferred_element_type=jnp.float32)


def dot_nn(a, b):
    return jnp.dot(a, b, preferred_element_type=jnp.float32)


def pause():
    def kernel(out_ref):
        out_ref[...] = jnp.zeros_like(out_ref)

    return pl.pallas_call(
        kernel,
        out_specs=pl.BlockSpec(memory_space=pltpu.VMEM),
        out_shape=pltpu.VMEM((8, 128), jnp.float32),
        cost_estimate=pl.CostEstimate(
            flops=PAUSE_FLOPS, bytes_accessed=PAUSE_BYTES, transcendentals=0
        ),
        name="pause",
    )()


def call(body, operands, in_specs, out_shape, scratch, bring, limit, flops, name, aliases=None):
    w_out, piece_rows, pieces = bring
    vmem, hbm = pl.BlockSpec(memory_space=pltpu.VMEM), pl.BlockSpec(memory_space=pltpu.HBM)
    n_in, n_out = len(operands), len(out_shape)
    copied = 0
    if pieces:
        operands, in_specs = [*operands, w_out], [*in_specs, hbm]
        out_shape = [*out_shape] + [pltpu.VMEM((piece_rows, w_out.shape[1]), w_out.dtype)] * len(pieces)
        scratch = [*scratch, pltpu.SemaphoreType.DMA((len(pieces),))]
        copied = 2 * len(pieces) * piece_rows * w_out.shape[1]

    def kernel(*refs):
        ins, rest = refs[: len(operands)], refs[len(operands) :]
        outs, rest = rest[: len(out_shape)], rest[len(out_shape) :]
        copies = []
        for i, piece in enumerate(pieces):
            rows = pl.ds(piece * piece_rows, piece_rows)
            copies.append(pltpu.make_async_copy(ins[-1].at[rows], outs[n_out + i], rest[-1].at[i]))
        for copy in copies:
            copy.start()
        body(ins[:n_in], outs[:n_out], rest[: len(scratch) - bool(pieces)])
        for copy in copies:
            copy.wait()

    out = pl.pallas_call(
        kernel,
        in_specs=in_specs,
        out_specs=[vmem] * len(out_shape),
        out_shape=out_shape,
        scratch_shapes=scratch,
        compiler_params=pltpu.CompilerParams(vmem_limit_bytes=limit * MIB),
        cost_estimate=pl.CostEstimate(
            flops=flops, bytes_accessed=4 * MIB + copied, transcendentals=0
        ),
        input_output_aliases=aliases or {},
        name=name,
    )(*operands)
    return out[:n_out], list(out[n_out:])


def update(scores, m, l, acc, probs_into):
    new_m = m
    for s in scores:
        new_m = jnp.maximum(new_m, jnp.max(s, axis=1, keepdims=True))
    shrink = jnp.exp2((m - new_m) * SCALE2)
    weights = [jnp.exp2((s - new_m) * SCALE2) for s in scores]
    l = l * shrink
    for p in weights:
        l += jnp.sum(p, axis=1, keepdims=True)
    return new_m, l, probs_into(acc * shrink, [p.astype(jnp.bfloat16) for p in weights])


def in_turn(tasks, score, finish, looped):
    def some(first, count):
        before = None
        for i in range(count):
            task = first + i
            now = score(task)
            if before is not None:
                finish(*before)
            before = (task, now)
        finish(*before)

    if tasks % 2 or not looped:
        some(0, tasks)
    else:

        @pl.loop(0, 2)
        def _(i):
            some(i * (tasks // 2), tasks // 2)


def near_call(paused, suffix_len, queries, suffix_t, new_latent, own, beside, units, axis_size, bring):
    rows, steps, heads, width = queries.shape
    tile = heads // units
    share = heads // axis_size
    per = steps * heads

    def body(ins, outs, _):
        _, len_buf, q_buf, suf_buf, new_buf, own_ref, beside_ref = ins
        qs_ref, m_ref, l_ref, acc_ref = outs
        keys = [own_ref[...], beside_ref[...]]

        def sort(r):
            by_unit = [[] for _ in range(units)]
            for s in range(steps):
                q = q_buf[r, s].astype(jnp.float32)
                for u in range(units):
                    picked = [
                        q[j * share + u * CHUNK_HEADS : j * share + (u + 1) * CHUNK_HEADS]
                        for j in range(axis_size)
                    ]
                    by_unit[u].append(jnp.concatenate(picked, axis=0).astype(jnp.bfloat16))
            for u in range(units):
                for s in range(steps):
                    qs_ref[u, r * steps + s] = by_unit[u][s]
            return jnp.concatenate([x for unit in by_unit for x in unit], axis=0)

        def score(task):
            first = task * (BLOCK // per)
            q = [sort(first + i) for i in range(BLOCK // per)]
            both = jnp.concatenate(q, axis=0)
            scores = [dot_nn(both, k) for k in keys]
            old, new = [], []
            for i, x in enumerate(q):
                s = dot_nn(x, suf_buf[first + i])
                at = lax.broadcasted_iota(jnp.int32, s.shape, 1)
                old.append(jnp.where(at < len_buf[first + i], s, NEG))
                s = dot_nt(x, new_buf[first + i])
                step = lax.broadcasted_iota(jnp.int32, s.shape, 0) // tile % steps
                token = lax.broadcasted_iota(jnp.int32, s.shape, 1)
                new.append(jnp.where(token <= step, s, NEG))
            return scores + [jnp.concatenate(x, axis=0) for x in (old, new)]

        def finish(task, scores):
            first = task * (BLOCK // per)
            m = functools.reduce(
                jnp.maximum, [jnp.max(s, axis=1, keepdims=True) for s in scores]
            )
            weights = [jnp.exp2((s - m) * SCALE2) for s in scores]
            l = sum(jnp.sum(p, axis=1, keepdims=True) for p in weights)
            probs = [p.astype(jnp.bfloat16) for p in weights]
            acc = dot_nt(probs[0], keys[0][:LATENT]) + dot_nt(probs[1], keys[1][:LATENT])
            new_probs = probs[3].astype(jnp.float32)
            for i in range(BLOCK // per):
                here = slice(i * per, (i + 1) * per)
                part = acc[here] + dot_nt(probs[2][here], suf_buf[first + i, :LATENT])
                values = new_buf[first + i][:, :LATENT].astype(jnp.float32)
                for t in range(steps):
                    part += new_probs[here, t : t + 1] * values[t : t + 1]
                there = pl.ds((first + i) * steps, steps)
                lead = (units, steps, tile)
                m_ref[:, there] = jnp.broadcast_to(m[here], (per, 128)).reshape(lead + (128,))
                l_ref[:, there] = jnp.broadcast_to(l[here], (per, 128)).reshape(lead + (128,))
                acc_ref[:, there] = part.reshape(lead + (LATENT,))

        in_turn(rows * per // BLOCK, score, finish, True)

    vmem, smem = pl.BlockSpec(memory_space=pltpu.VMEM), pl.BlockSpec(memory_space=pltpu.SMEM)
    lead = (units, rows * steps, tile)
    f32 = jnp.float32
    return call(
        body,
        [paused, suffix_len, queries, suffix_t, new_latent, own, beside],
        [vmem, smem] + [vmem] * 5,
        [
            jax.ShapeDtypeStruct(lead + (width,), queries.dtype),
            jax.ShapeDtypeStruct(lead + (128,), f32),
            jax.ShapeDtypeStruct(lead + (128,), f32),
            jax.ShapeDtypeStruct(lead + (LATENT,), f32),
        ],
        [],
        bring,
        NEAR_LIMIT,
        4 * rows * per * 1100 * 768,
        "near_attention",
    )


def merge(first, size, keys, q_ref, m_ref, l_ref, acc_ref, store, looped):
    _, pairs, tile, width = q_ref.shape
    step = BLOCK // tile
    blocks = pairs // step

    def at(task):
        return first + task // blocks, pl.ds(task % blocks * step, step)

    def score(task):
        here = at(task)
        q = q_ref[here].reshape(BLOCK, width)
        return [dot_nn(q, k) for k in keys]

    def finish(task, scores):
        here = at(task)
        store(
            task,
            here,
            *update(
                scores,
                m_ref[here].reshape(BLOCK, 128)[:, 0:1],
                l_ref[here].reshape(BLOCK, 128)[:, 0:1],
                acc_ref[here].reshape(BLOCK, LATENT),
                lambda acc, ps: acc + sum(dot_nt(p, k[:LATENT]) for p, k in zip(ps, keys)),
            ),
        )

    in_turn(size * blocks, score, finish, looped)


def middle_call(queries, state, keys, bring):
    units, pairs, tile, _ = queries.shape

    def body(ins, outs, _):
        q_ref, m_ref, l_ref, acc_ref, *key_refs = ins
        m_out, l_out, acc_out = outs

        def store(task, here, m, l, acc):
            lead = (BLOCK // tile, tile)
            m_out[here] = jnp.broadcast_to(m, (BLOCK, 128)).reshape(lead + (128,))
            l_out[here] = jnp.broadcast_to(l, (BLOCK, 128)).reshape(lead + (128,))
            acc_out[here] = acc.reshape(lead + (LATENT,))

        merge(0, units, [k[...] for k in key_refs], q_ref, m_ref, l_ref, acc_ref, store, True)

    operands = [queries, *state, *keys]
    return call(
        body,
        operands,
        [pl.BlockSpec(memory_space=pltpu.VMEM)] * len(operands),
        [jax.ShapeDtypeStruct(x.shape, x.dtype) for x in state],
        [],
        bring,
        28 if bring[2] else 10,
        2 * units * pairs * tile * 1100 * 256 * len(keys),
        "middle_attention",
    )


def far_call(first, size, queries, state, keys, axis_size, bring):
    _, pairs, tile, _ = queries.shape
    per_unit = pairs * tile

    def body(ins, out_refs, scratch):
        q_ref, m_ref, l_ref, acc_ref, *key_refs = ins
        (done,) = scratch

        def store(task, here, m, l, acc):
            attended = acc / l
            rows = pl.ds(task * BLOCK, BLOCK)
            for g in range(LATENT // 128):
                done[g, rows, :] = attended[:, g * 128 : (g + 1) * 128]

        keys_now = [k[...] for k in key_refs]
        merge(first, size, keys_now, q_ref, m_ref, l_ref, acc_ref, store, bool(bring[2]))
        me = lax.axis_index("roll")
        for k in range(axis_size):
            there = jnp.bitwise_xor(me, k) * CHUNK_HEADS
            for u in range(size):
                for i in range(CHUNK_HEADS):
                    at = (u * CHUNK_HEADS + i) * pairs
                    for g in range(LATENT // 128):
                        out_refs[k][at : at + pairs, g * 128 : (g + 1) * 128] = done[
                            g, pl.ds(u * per_unit + there + i, pairs, stride=tile), :
                        ].astype(jnp.bfloat16)

    operands = [queries, *state, *keys]
    return call(
        body,
        operands,
        [pl.BlockSpec(memory_space=pltpu.VMEM)] * len(operands),
        [jax.ShapeDtypeStruct((size * CHUNK_HEADS * pairs, LATENT), jnp.bfloat16)] * axis_size,
        [pltpu.VMEM((LATENT // 128, size * per_unit + tile, 128), jnp.float32)],
        bring,
        FAR_LIMIT if bring[2] else 8,
        2 * size * per_unit * 1100 * 256 * len(keys),
        "far_attention",
    )


def project(first_head, heads, pieces, acc, w_uv, w_pieces, bring, kept=None, first_col=0, cols=None):
    pairs = pieces[0].shape[0] // heads
    total_rows = len(pieces) * pairs
    piece_rows, width = w_pieces[0].shape
    cols = width if cols is None else cols
    block = next(b for b in (1792, 1024, 896, 512, 128) if cols % b == 0)

    def body(ins, outs, _):
        ins = list(ins)
        piece_refs = [ins.pop(0) for _ in pieces]
        acc_ref = ins.pop(0) if acc is not None else None
        uv_ref, *w_refs = ins
        head_out = []
        for i in range(heads):
            rows = jnp.concatenate([p[i * pairs : (i + 1) * pairs, :] for p in piece_refs], axis=0)
            head_out.append(dot_nn(rows, uv_ref[first_head + i]).astype(jnp.bfloat16))
        head_out = jnp.concatenate(head_out, axis=1)

        def block_of(b):
            here = pl.ds(b * block, block)
            there = pl.ds(first_col + b * block, block)
            total = sum(
                dot_nn(head_out[:, i * piece_rows : (i + 1) * piece_rows], w_ref[:, there])
                for i, w_ref in enumerate(w_refs)
            )
            if acc_ref is not None:
                total += acc_ref[:, there]
            if kept is None:
                outs[0][:, here] = total
                return
            at = [0, 0]
            for k in range(len(pieces)):
                side = 0 if k in kept else 1
                outs[side][at[side] * pairs : (at[side] + 1) * pairs, here] = total[
                    k * pairs : (k + 1) * pairs
                ].astype(jnp.bfloat16)
                at[side] += 1

        if bring[2]:
            pl.loop(0, cols // block)(block_of)
        else:
            for b in range(cols // block):
                block_of(b)

    operands = [*pieces] + ([acc] if acc is not None else []) + [w_uv, *w_pieces]
    if kept is not None:
        out_shape = [jax.ShapeDtypeStruct((total_rows // 2, cols), jnp.bfloat16)] * 2
    else:
        out_shape = [jax.ShapeDtypeStruct((total_rows, cols), jnp.float32)]
    return call(
        body,
        operands,
        [pl.BlockSpec(memory_space=pltpu.VMEM)] * len(operands),
        out_shape,
        [],
        bring,
        PROJECT_LIMIT if bring[2] else 8,
        8 * total_rows * heads * w_uv.shape[2] * cols,
        "project",
        {len(pieces): 0} if acc is not None and kept is None else {},
    )


def last_sums(rows, steps, width, parts):
    pairs = rows * steps
    flat = [x for part in parts for x in part]
    cols = width // len(parts)

    def kernel(*refs):
        refs, out_ref = list(refs[:-1]), refs[-1]
        for i, part in enumerate(parts):
            total = None
            for _, first in part:
                x = refs.pop(0)[first : first + pairs, :].astype(jnp.float32)
                total = x if total is None else total + x
            out_ref[:, :, i * cols : (i + 1) * cols] = total.astype(jnp.bfloat16).reshape(
                rows, steps, cols
            )

    vmem = pl.BlockSpec(memory_space=pltpu.VMEM)
    return pl.pallas_call(
        kernel,
        in_specs=[vmem] * len(flat),
        out_specs=vmem,
        out_shape=jax.ShapeDtypeStruct((rows, steps, width), jnp.bfloat16),
        compiler_params=pltpu.CompilerParams(vmem_limit_bytes=8 * MIB),
        name="last_sums",
    )(*[x for x, _ in flat])


def on_device(prefix_latent, suffix_latent, suffix_len, new_latent, queries, w_uv, w_out):
    n = lax.axis_size("roll")
    rows, steps, heads, _ = queries.shape
    pairs = rows * steps
    width = w_out.shape[1]
    share = heads // n
    units = share // CHUNK_HEADS
    chunks = [(0, units // 2), (units // 2, units - units // 2)] if units > 1 else [(0, 1)]
    piece_rows = CHUNK_HEADS * w_uv.shape[2] // W_PIECES
    n_pieces = units * W_PIECES
    half = n_pieces // 2
    brings = {"near": list(range(half))}
    if len(chunks) > 1:
        brings["far", 1] = list(range(half, half + half // 4))
        brings["project", 0] = list(range(half + half // 4, n_pieces))
    else:
        brings["middle"] = list(range(half, n_pieces))
    held = {}

    def bring(who):
        return (w_out, piece_rows, brings.get(who, []))

    def keep(who, result):
        out, brought = result
        held.update(zip(brings.get(who, []), brought))
        return out

    def swap(x, k):
        return lax.ppermute(x, "roll", [(i, i ^ k) for i in range(n)])

    own = prefix_latent.T.astype(jnp.bfloat16)
    own, paused = lax.optimization_barrier((own, pause()))
    across = [swap(own, k) for k in range(2, n, 2)]
    beside = swap(own, 1)
    queries, m, l, acc = keep(
        "near",
        near_call(
            paused,
            suffix_len,
            queries,
            jnp.swapaxes(suffix_latent, 1, 2),
            new_latent,
            own,
            beside,
            units,
            n,
            bring("near"),
        ),
    )
    *across, m = lax.optimization_barrier((*across, m))
    forwarded = [swap(x, 1) for x in across]
    state = keep("middle", middle_call(queries, (m, l, acc), across, bring("middle")))
    got = []
    for c, (first, size) in enumerate(chunks):
        who = ("far", c)
        mine = keep(who, far_call(first, size, queries, state, forwarded, n, bring(who)))
        *mine, queries = lax.optimization_barrier((*mine, queries))
        there = [mine[0]] + [None] * (n - 1)
        for k in [*range(2, n), 1]:
            there[k] = swap(mine[k], k)
        got.append(there)
    acc = None

    def pieces_of(first, size):
        return [held[i] for i in range(first * W_PIECES, (first + size) * W_PIECES)]

    for c, (first, size) in enumerate(chunks[:-1]):
        who = ("project", c)
        (acc,) = keep(
            who,
            project(
                first * CHUNK_HEADS,
                size * CHUNK_HEADS,
                got[c],
                acc,
                w_uv,
                pieces_of(first, size),
                bring(who),
            ),
        )
    first, size = chunks[-1]
    cols = width // OUT_PARTS
    parts = []
    for part in range(OUT_PARTS):
        odd = part % 2
        kept = tuple(k for k in range(n) if k == 0 or (k != 1 and k % 2 == odd))
        (stay, send), _ = project(
            first * CHUNK_HEADS,
            size * CHUNK_HEADS,
            got[-1],
            acc,
            w_uv,
            pieces_of(first, size),
            bring(None),
            kept,
            part * cols,
            cols,
        )
        left = [k for k in range(n) if k not in kept]
        recv = swap(send, 1)

        def piece(x, i):
            return x[i * pairs : (i + 1) * pairs].astype(jnp.float32)

        terms = [(stay, 0), (recv, left.index(1) * pairs)]
        for i, k in enumerate(kept[1:]):
            both = piece(stay, i + 1) + piece(recv, left.index(k ^ 1))
            terms.append((swap(both.astype(jnp.bfloat16), k), 0))
        parts.append(terms)
    return last_sums(rows, steps, width, parts)


def solution(mesh):
    in_specs = (
        P(("group", "roll"), None),
        P(("group", "roll"), None, None),
        P(("group", "roll")),
        P(("group", "roll"), None, None),
        P(("group", "roll"), None, None, None),
        P("roll", None, None),
        P("roll", None),
    )
    out_specs = P(("group", "roll"), None, None)
    return jax.shard_map(
        on_device, mesh=mesh, in_specs=in_specs, out_specs=out_specs, check_vma=False
    )
```

```python
import functools
import math

import jax
import jax.numpy as jnp
from jax import lax
from jax.experimental import pallas as pl
from jax.experimental.pallas import tpu as pltpu
from jax.sharding import PartitionSpec as P

LATENT = 512
QK_HEAD = 192
SCALE2 = QK_HEAD**-0.5 * math.log2(math.e)
NEG = -1e30
CHUNK_HEADS = 4
OUT_PARTS = 2
BLOCK = 256
K_STEP = 256
MIB = 2**20
NEAR_LIMIT = 20
FAR_LIMIT = 20
PROJECT_LIMIT = 10
PAUSE_FLOPS = 10**10
PAUSE_BYTES = 30 * MIB


def dot_nt(a, b):
    return lax.dot_general(a, b, (((1,), (1,)), ((), ())), preferred_element_type=jnp.float32)


def dot_nn(a, b):
    return jnp.dot(a, b, preferred_element_type=jnp.float32)


def pause():
    def kernel(out_ref):
        out_ref[...] = jnp.zeros_like(out_ref)

    return pl.pallas_call(
        kernel,
        out_specs=pl.BlockSpec(memory_space=pltpu.VMEM),
        out_shape=pltpu.VMEM((8, 128), jnp.float32),
        cost_estimate=pl.CostEstimate(
            flops=PAUSE_FLOPS, bytes_accessed=PAUSE_BYTES, transcendentals=0
        ),
        name="pause",
    )()


def call(body, operands, in_specs, out_shape, scratch, bring, limit, flops, name, aliases=None):
    w_out, pieces = bring
    vmem, hbm = pl.BlockSpec(memory_space=pltpu.VMEM), pl.BlockSpec(memory_space=pltpu.HBM)
    n_in, n_out = len(operands), len(out_shape)
    copied = 0
    if pieces:
        operands, in_specs = [*operands, w_out], [*in_specs, hbm]
        out_shape = [*out_shape]
        out_shape += [pltpu.VMEM((count, w_out.shape[1]), w_out.dtype) for _, count in pieces]
        scratch = [*scratch, pltpu.SemaphoreType.DMA((len(pieces),))]
        copied = 2 * sum(count for _, count in pieces) * w_out.shape[1]

    def kernel(*refs):
        ins, rest = refs[: len(operands)], refs[len(operands) :]
        outs, rest = rest[: len(out_shape)], rest[len(out_shape) :]
        copies = []
        for i, piece in enumerate(pieces):
            copies.append(pltpu.make_async_copy(ins[-1].at[pl.ds(*piece)], outs[n_out + i], rest[-1].at[i]))
        for copy in copies:
            copy.start()
        body(ins[:n_in], outs[:n_out], rest[: len(scratch) - bool(pieces)])
        for copy in copies:
            copy.wait()

    out = pl.pallas_call(
        kernel,
        in_specs=in_specs,
        out_specs=[vmem] * len(out_shape),
        out_shape=out_shape,
        scratch_shapes=scratch,
        compiler_params=pltpu.CompilerParams(vmem_limit_bytes=limit * MIB),
        cost_estimate=pl.CostEstimate(
            flops=flops, bytes_accessed=4 * MIB + copied, transcendentals=0
        ),
        input_output_aliases=aliases or {},
        name=name,
    )(*operands)
    return out[:n_out], list(out[n_out:])


def update(scores, m, l, acc, probs_into):
    new_m = m
    for s in scores:
        new_m = jnp.maximum(new_m, jnp.max(s, axis=1, keepdims=True))
    shrink = jnp.exp2((m - new_m) * SCALE2)
    weights = [jnp.exp2((s - new_m) * SCALE2) for s in scores]
    l = l * shrink
    for p in weights:
        l += jnp.sum(p, axis=1, keepdims=True)
    return new_m, l, probs_into(acc * shrink, [p.astype(jnp.bfloat16) for p in weights])


def in_turn(tasks, score, finish, looped):
    def some(first, count):
        before = None
        for i in range(count):
            task = first + i
            now = score(task)
            if before is not None:
                finish(*before)
            before = (task, now)
        finish(*before)

    if tasks % 2 or not looped:
        some(0, tasks)
    else:

        @pl.loop(0, 2)
        def _(i):
            some(i * (tasks // 2), tasks // 2)


def near_call(paused, suffix_len, queries, suffix_t, new_latent, own, units, axis_size, bring):
    rows, steps, heads, width = queries.shape
    tile = heads // units
    share = heads // axis_size
    per = steps * heads

    def body(ins, outs, _):
        _, len_buf, q_buf, suf_buf, new_buf, own_ref = ins
        qs_ref, m_ref, l_ref, acc_ref = outs
        keys = own_ref[...]

        def sort(r):
            by_unit = [[] for _ in range(units)]
            for s in range(steps):
                q = q_buf[r, s].astype(jnp.float32)
                for u in range(units):
                    picked = [
                        q[j * share + u * CHUNK_HEADS : j * share + (u + 1) * CHUNK_HEADS]
                        for j in range(axis_size)
                    ]
                    by_unit[u].append(jnp.concatenate(picked, axis=0).astype(jnp.bfloat16))
            for u in range(units):
                for s in range(steps):
                    qs_ref[u, r * steps + s] = by_unit[u][s]
            return jnp.concatenate([x for unit in by_unit for x in unit], axis=0)

        def score(task):
            first = task * (BLOCK // per)
            q = [sort(first + i) for i in range(BLOCK // per)]
            both = jnp.concatenate(q, axis=0)
            scores = [dot_nn(both, keys)]
            old, new = [], []
            for i, x in enumerate(q):
                s = dot_nn(x, suf_buf[first + i])
                at = lax.broadcasted_iota(jnp.int32, s.shape, 1)
                old.append(jnp.where(at < len_buf[first + i], s, NEG))
                s = dot_nt(x, new_buf[first + i])
                step = lax.broadcasted_iota(jnp.int32, s.shape, 0) // tile % steps
                token = lax.broadcasted_iota(jnp.int32, s.shape, 1)
                new.append(jnp.where(token <= step, s, NEG))
            return scores + [jnp.concatenate(x, axis=0) for x in (old, new)]

        def finish(task, scores):
            first = task * (BLOCK // per)
            m = functools.reduce(
                jnp.maximum, [jnp.max(s, axis=1, keepdims=True) for s in scores]
            )
            weights = [jnp.exp2((s - m) * SCALE2) for s in scores]
            l = sum(jnp.sum(p, axis=1, keepdims=True) for p in weights)
            probs = [p.astype(jnp.bfloat16) for p in weights]
            acc = dot_nt(probs[0], keys[:LATENT])
            new_probs = probs[2].astype(jnp.float32)
            for i in range(BLOCK // per):
                here = slice(i * per, (i + 1) * per)
                part = acc[here] + dot_nt(probs[1][here], suf_buf[first + i, :LATENT])
                values = new_buf[first + i][:, :LATENT].astype(jnp.float32)
                for t in range(steps):
                    part += new_probs[here, t : t + 1] * values[t : t + 1]
                there = pl.ds((first + i) * steps, steps)
                lead = (units, steps, tile)
                m_ref[:, there] = jnp.broadcast_to(m[here], (per, 128)).reshape(lead + (128,))
                l_ref[:, there] = jnp.broadcast_to(l[here], (per, 128)).reshape(lead + (128,))
                acc_ref[:, there] = part.reshape(lead + (LATENT,))

        in_turn(rows * per // BLOCK, score, finish, True)

    vmem, smem = pl.BlockSpec(memory_space=pltpu.VMEM), pl.BlockSpec(memory_space=pltpu.SMEM)
    lead = (units, rows * steps, tile)
    f32 = jnp.float32
    return call(
        body,
        [paused, suffix_len, queries, suffix_t, new_latent, own],
        [vmem, smem] + [vmem] * 4,
        [
            jax.ShapeDtypeStruct(lead + (width,), queries.dtype),
            jax.ShapeDtypeStruct(lead + (128,), f32),
            jax.ShapeDtypeStruct(lead + (128,), f32),
            jax.ShapeDtypeStruct(lead + (LATENT,), f32),
        ],
        [],
        bring,
        NEAR_LIMIT,
        rows * per * 1100 * 768,
        "near_attention",
    )


def merge(first, size, keys, q_ref, m_ref, l_ref, acc_ref, store, looped):
    _, pairs, tile, width = q_ref.shape
    step = BLOCK // tile
    blocks = pairs // step

    def at(task):
        return first + task // blocks, pl.ds(task % blocks * step, step)

    def score(task):
        here = at(task)
        q = q_ref[here].reshape(BLOCK, width)
        return [dot_nn(q, k) for k in keys]

    def finish(task, scores):
        here = at(task)
        store(
            task,
            here,
            *update(
                scores,
                m_ref[here].reshape(BLOCK, 128)[:, 0:1],
                l_ref[here].reshape(BLOCK, 128)[:, 0:1],
                acc_ref[here].reshape(BLOCK, LATENT),
                lambda acc, ps: acc + sum(dot_nt(p, k[:LATENT]) for p, k in zip(ps, keys)),
            ),
        )

    in_turn(size * blocks, score, finish, looped)


def middle_call(units, queries, state, keys, bring):
    _, pairs, tile, _ = queries.shape

    def body(ins, outs, _):
        q_ref, m_ref, l_ref, acc_ref, *key_refs = ins
        m_out, l_out, acc_out = outs

        def store(task, here, m, l, acc):
            lead = (BLOCK // tile, tile)
            m_out[here] = jnp.broadcast_to(m, (BLOCK, 128)).reshape(lead + (128,))
            l_out[here] = jnp.broadcast_to(l, (BLOCK, 128)).reshape(lead + (128,))
            acc_out[here] = acc.reshape(lead + (LATENT,))

        merge(0, units, [k[...] for k in key_refs], q_ref, m_ref, l_ref, acc_ref, store, bool(bring[1]))

    operands = [queries, *state, *keys]
    return call(
        body,
        operands,
        [pl.BlockSpec(memory_space=pltpu.VMEM)] * len(operands),
        [jax.ShapeDtypeStruct((units,) + x.shape[1:], x.dtype) for x in state],
        [],
        bring,
        28 if bring[1] else 10,
        2 * units * pairs * tile * 1100 * 256 * len(keys),
        "middle_attention",
    )


def far_call(first, size, queries, state, keys, axis_size, bring):
    _, pairs, tile, _ = queries.shape
    per_unit = pairs * tile

    def body(ins, out_refs, scratch):
        q_ref, m_ref, l_ref, acc_ref, *key_refs = ins
        (done,) = scratch

        me = lax.axis_index("roll")

        def part(u):
            for k in range(axis_size):
                there = u * per_unit + jnp.bitwise_xor(me, k) * CHUNK_HEADS
                for i in range(CHUNK_HEADS):
                    at = pl.ds(pl.multiple_of((u * CHUNK_HEADS + i) * pairs, pairs), pairs)
                    for g in range(LATENT // 128):
                        out_refs[k][at, g * 128 : (g + 1) * 128] = done[
                            g, pl.ds(there + i, pairs, stride=tile), :
                        ].astype(jnp.bfloat16)

        def store(task, here, m, l, acc):
            attended = acc * (1.0 / l)
            rows = pl.ds(task * BLOCK, BLOCK)
            for g in range(LATENT // 128):
                done[g, rows, :] = attended[:, g * 128 : (g + 1) * 128]
            if per_unit == BLOCK:
                part(task)

        keys_now = [k[...] for k in key_refs]
        merge(first, size, keys_now, q_ref, m_ref, l_ref, acc_ref, store, bool(bring[1]))
        if per_unit != BLOCK:
            for u in range(size):
                part(u)

    operands = [queries, *state, *keys]
    return call(
        body,
        operands,
        [pl.BlockSpec(memory_space=pltpu.VMEM)] * len(operands),
        [jax.ShapeDtypeStruct((size * CHUNK_HEADS * pairs, LATENT), jnp.bfloat16)] * axis_size,
        [pltpu.VMEM((LATENT // 128, size * per_unit + tile, 128), jnp.float32)],
        bring,
        FAR_LIMIT if bring[1] else 8,
        2 * size * per_unit * 1100 * 256 * len(keys),
        "far_attention",
    )


def project(first_head, heads, pieces, acc, w_uv, w_pieces, bring, kept=None, first_col=0, cols=None):
    pairs = pieces[0].shape[0] // heads
    total_rows = len(pieces) * pairs
    cols = w_pieces[0].shape[1] if cols is None else cols
    block = next(b for b in (1792, 1024, 896, 512, 128) if cols % b == 0)

    def body(ins, outs, _):
        ins = list(ins)
        piece_refs = [ins.pop(0) for _ in pieces]
        acc_ref = ins.pop(0) if acc is not None else None
        uv_ref, *w_refs = ins
        head_out = []
        for i in range(heads):
            rows = jnp.concatenate([p[i * pairs : (i + 1) * pairs, :] for p in piece_refs], axis=0)
            head_out.append(dot_nn(rows, uv_ref[first_head + i]).astype(jnp.bfloat16))
        head_out = jnp.concatenate(head_out, axis=1)

        def block_of(b):
            here = pl.ds(b * block, block)
            there = pl.ds(first_col + b * block, block)
            total, at = 0.0, 0
            for w_ref in w_refs:
                for row in range(0, w_ref.shape[0], K_STEP):
                    rows = slice(row, row + K_STEP)
                    total += dot_nn(head_out[:, at : at + K_STEP], w_ref[rows, there])
                    at += K_STEP
            if acc_ref is not None:
                total += acc_ref[:, there]
            if kept is None:
                outs[0][:, here] = total
                return
            at = [0, 0]
            for k in range(len(pieces)):
                side = 0 if k in kept else 1
                outs[side][at[side] * pairs : (at[side] + 1) * pairs, here] = total[
                    k * pairs : (k + 1) * pairs
                ].astype(jnp.bfloat16)
                at[side] += 1

        if bring[1]:
            pl.loop(0, cols // block)(block_of)
        else:
            for b in range(cols // block):
                block_of(b)

    operands = [*pieces] + ([acc] if acc is not None else []) + [w_uv, *w_pieces]
    if kept is not None:
        out_shape = [jax.ShapeDtypeStruct((total_rows // 2, cols), jnp.bfloat16)] * 2
    else:
        out_shape = [jax.ShapeDtypeStruct((total_rows, cols), jnp.float32)]
    return call(
        body,
        operands,
        [pl.BlockSpec(memory_space=pltpu.VMEM)] * len(operands),
        out_shape,
        [],
        bring,
        PROJECT_LIMIT if bring[1] else 8,
        8 * total_rows * heads * w_uv.shape[2] * cols,
        "project",
        {len(pieces): 0} if acc is not None and kept is None else {},
    )


def last_sums(shape, first_col, terms, so_far):
    rows, steps, _ = shape
    pairs = rows * steps
    cols = terms[0][0].shape[1]

    def kernel(*refs):
        out_ref, buf, sem = refs[-3:]
        total = None
        for ref, (_, first) in zip(refs, terms):
            x = ref[first : first + pairs, :].astype(jnp.float32)
            total = x if total is None else total + x
        buf[...] = total.astype(jnp.bfloat16).reshape(rows, steps, cols)
        copy = pltpu.make_async_copy(buf, out_ref.at[:, :, pl.ds(first_col, cols)], sem)
        copy.start()
        copy.wait()

    vmem, hbm = pl.BlockSpec(memory_space=pltpu.VMEM), pl.BlockSpec(memory_space=pltpu.HBM)
    held = [] if so_far is None else [so_far]
    return pl.pallas_call(
        kernel,
        in_specs=[vmem] * len(terms) + [hbm] * len(held),
        out_specs=hbm,
        out_shape=jax.ShapeDtypeStruct(shape, jnp.bfloat16),
        scratch_shapes=[pltpu.VMEM((rows, steps, cols), jnp.bfloat16), pltpu.SemaphoreType.DMA],
        input_output_aliases={len(terms): 0} if held else {},
        compiler_params=pltpu.CompilerParams(vmem_limit_bytes=8 * MIB),
        name="last_sums",
    )(*[x for x, _ in terms], *held)


def on_device(prefix_latent, suffix_latent, suffix_len, new_latent, queries, w_uv, w_out):
    n = lax.axis_size("roll")
    rows, steps, heads, _ = queries.shape
    pairs = rows * steps
    width = w_out.shape[1]
    share = heads // n
    units = share // CHUNK_HEADS
    chunks = [(0, units // 2), (units // 2, units - units // 2)] if units > 1 else [(0, 1)]
    depth = w_out.shape[0]
    half, eighth = depth // 2, depth // 8
    if len(chunks) > 1:
        brings = {
            "near": [(0, half - eighth)],
            ("far", 1): [(half - eighth, eighth)],
            ("project", 0): [(half, depth - half)],
        }
    else:
        brings = {"near": [(0, half)], "middle": [(half, depth - half)]}
    held = {}

    def bring(who):
        return (w_out, brings.get(who, []))

    def keep(who, result):
        out, brought = result
        held.update(zip(brings.get(who, []), brought))
        return out

    def swap(x, k):
        return lax.ppermute(x, "roll", [(i, i ^ k) for i in range(n)])

    own = prefix_latent.T.astype(jnp.bfloat16)
    own, paused = lax.optimization_barrier((own, pause()))
    across = [swap(own, k) for k in range(2, n, 2)]
    beside = swap(own, 1)
    queries, m, l, acc = keep(
        "near",
        near_call(
            paused,
            suffix_len,
            queries,
            jnp.swapaxes(suffix_latent, 1, 2),
            new_latent,
            own,
            units,
            n,
            bring("near"),
        ),
    )
    *across, m = lax.optimization_barrier((*across, m))
    forwarded = [swap(x, 1) for x in across]
    state = (m, l, acc)
    middle = keep("middle", middle_call(chunks[0][1], queries, state, [beside] + across, bring("middle")))
    got = []
    for c, (first, size) in enumerate(chunks):
        who = ("far", c)
        if c == 0:
            result = far_call(first, size, queries, middle, forwarded, n, bring(who))
        else:
            result = far_call(first, size, queries, state, [beside] + across + forwarded, n, bring(who))
        mine = keep(who, result)
        *mine, queries = lax.optimization_barrier((*mine, queries))
        there = [mine[0]] + [None] * (n - 1)
        for k in [*range(2, n), 1]:
            there[k] = swap(mine[k], k)
        got.append(there)
    acc = None

    def pieces_of(first, size):
        unit_rows = depth // units
        first, end = first * unit_rows, (first + size) * unit_rows
        return [held[piece] for piece in sorted(held) if first <= piece[0] < end]

    for c, (first, size) in enumerate(chunks[:-1]):
        who = ("project", c)
        (acc,) = keep(
            who,
            project(
                first * CHUNK_HEADS,
                size * CHUNK_HEADS,
                got[c],
                acc,
                w_uv,
                pieces_of(first, size),
                bring(who),
            ),
        )
    first, size = chunks[-1]
    cols = width // OUT_PARTS
    parts = []
    for part in range(OUT_PARTS):
        odd = part % 2
        kept = tuple(k for k in range(n) if k == 0 or (k != 1 and k % 2 == odd))
        (stay, send), _ = project(
            first * CHUNK_HEADS,
            size * CHUNK_HEADS,
            got[-1],
            acc,
            w_uv,
            pieces_of(first, size),
            bring(None),
            kept,
            part * cols,
            cols,
        )
        left = [k for k in range(n) if k not in kept]
        recv = swap(send, 1)

        def piece(x, i):
            return x[i * pairs : (i + 1) * pairs].astype(jnp.float32)

        terms = [(stay, 0), (recv, left.index(1) * pairs)]
        for i, k in enumerate(kept[1:]):
            both = piece(stay, i + 1) + piece(recv, left.index(k ^ 1))
            terms.append((swap(both.astype(jnp.bfloat16), k), 0))
        parts.append(terms)
    out = None
    for part, terms in enumerate(parts):
        out = last_sums((rows, steps, width), part * cols, terms, out)
    return out


def solution(mesh):
    in_specs = (
        P(("group", "roll"), None),
        P(("group", "roll"), None, None),
        P(("group", "roll")),
        P(("group", "roll"), None, None),
        P(("group", "roll"), None, None, None),
        P("roll", None, None),
        P("roll", None),
    )
    out_specs = P(("group", "roll"), None, None)
    return jax.shard_map(
        on_device, mesh=mesh, in_specs=in_specs, out_specs=out_specs, check_vma=False
    )
```

```python
import functools
import math

import jax
import jax.numpy as jnp
from jax import lax
from jax.experimental import pallas as pl
from jax.experimental.pallas import tpu as pltpu
from jax.sharding import PartitionSpec as P

LATENT = 512
QK_HEAD = 192
SCALE2 = QK_HEAD**-0.5 * math.log2(math.e)
NEG = -1e30
CHUNK_HEADS = 4
OUT_PARTS = 2
BLOCK = 256
K_STEP = 256
MIB = 2**20
NEAR_LIMIT = 20
FAR_LIMIT = 20
PROJECT_LIMIT = 10
PAUSE_FLOPS = 10**10
PAUSE_BYTES = 30 * MIB


def dot_nt(a, b):
    return lax.dot_general(a, b, (((1,), (1,)), ((), ())), preferred_element_type=jnp.float32)


def dot_nn(a, b):
    return jnp.dot(a, b, preferred_element_type=jnp.float32)


def pause():
    def kernel(out_ref):
        out_ref[...] = jnp.zeros_like(out_ref)

    return pl.pallas_call(
        kernel,
        out_specs=pl.BlockSpec(memory_space=pltpu.VMEM),
        out_shape=pltpu.VMEM((8, 128), jnp.float32),
        cost_estimate=pl.CostEstimate(
            flops=PAUSE_FLOPS, bytes_accessed=PAUSE_BYTES, transcendentals=0
        ),
        name="pause",
    )()


def call(body, operands, in_specs, out_shape, scratch, bring, limit, flops, name, aliases=None):
    w_out, pieces = bring
    vmem, hbm = pl.BlockSpec(memory_space=pltpu.VMEM), pl.BlockSpec(memory_space=pltpu.HBM)
    n_in, n_out = len(operands), len(out_shape)
    copied = 0
    if pieces:
        operands, in_specs = [*operands, w_out], [*in_specs, hbm]
        out_shape = [*out_shape]
        out_shape += [pltpu.VMEM((count, w_out.shape[1]), w_out.dtype) for _, count in pieces]
        scratch = [*scratch, pltpu.SemaphoreType.DMA((len(pieces),))]
        copied = 2 * sum(count for _, count in pieces) * w_out.shape[1]

    def kernel(*refs):
        ins, rest = refs[: len(operands)], refs[len(operands) :]
        outs, rest = rest[: len(out_shape)], rest[len(out_shape) :]
        copies = []
        for i, piece in enumerate(pieces):
            copies.append(pltpu.make_async_copy(ins[-1].at[pl.ds(*piece)], outs[n_out + i], rest[-1].at[i]))
        for copy in copies:
            copy.start()
        body(ins[:n_in], outs[:n_out], rest[: len(scratch) - bool(pieces)])
        for copy in copies:
            copy.wait()

    out = pl.pallas_call(
        kernel,
        in_specs=in_specs,
        out_specs=[vmem] * len(out_shape),
        out_shape=out_shape,
        scratch_shapes=scratch,
        compiler_params=pltpu.CompilerParams(vmem_limit_bytes=limit * MIB),
        cost_estimate=pl.CostEstimate(
            flops=flops, bytes_accessed=4 * MIB + copied, transcendentals=0
        ),
        input_output_aliases=aliases or {},
        name=name,
    )(*operands)
    return out[:n_out], list(out[n_out:])


def update(scores, m, l, acc, probs_into):
    new_m = m
    for s in scores:
        new_m = jnp.maximum(new_m, jnp.max(s, axis=1, keepdims=True))
    shrink = jnp.exp2((m - new_m) * SCALE2)
    weights = [jnp.exp2((s - new_m) * SCALE2) for s in scores]
    l = l * shrink
    for p in weights:
        l += jnp.sum(p, axis=1, keepdims=True)
    return new_m, l, probs_into(acc * shrink, [p.astype(jnp.bfloat16) for p in weights])


def in_turn(tasks, score, finish, looped):
    def some(first, count):
        before = None
        for i in range(count):
            task = first + i
            now = score(task)
            if before is not None:
                finish(*before)
            before = (task, now)
        finish(*before)

    if tasks % 2 or not looped:
        some(0, tasks)
    else:

        @pl.loop(0, 2)
        def _(i):
            some(i * (tasks // 2), tasks // 2)


def near_call(paused, suffix_len, queries, suffix_t, new_latent, own, units, axis_size, bring):
    rows, steps, heads, width = queries.shape
    tile = heads // units
    share = heads // axis_size
    per = steps * heads

    def body(ins, outs, _):
        _, len_buf, q_buf, suf_buf, new_buf, own_ref = ins
        qs_ref, m_ref, l_ref, acc_ref = outs
        keys = own_ref[...]

        def sort(r):
            by_unit = [[] for _ in range(units)]
            for s in range(steps):
                q = q_buf[r, s].astype(jnp.float32)
                for u in range(units):
                    picked = [
                        q[j * share + u * CHUNK_HEADS : j * share + (u + 1) * CHUNK_HEADS]
                        for j in range(axis_size)
                    ]
                    by_unit[u].append(jnp.concatenate(picked, axis=0).astype(jnp.bfloat16))
            for u in range(units):
                for s in range(steps):
                    qs_ref[u, r * steps + s] = by_unit[u][s]
            return jnp.concatenate([x for unit in by_unit for x in unit], axis=0)

        def score(task):
            first = task * (BLOCK // per)
            q = [sort(first + i) for i in range(BLOCK // per)]
            both = jnp.concatenate(q, axis=0)
            scores = [dot_nn(both, keys)]
            old, new = [], []
            for i, x in enumerate(q):
                s = dot_nn(x, suf_buf[first + i])
                at = lax.broadcasted_iota(jnp.int32, s.shape, 1)
                old.append(jnp.where(at < len_buf[first + i], s, NEG))
                s = dot_nt(x, new_buf[first + i])
                step = lax.broadcasted_iota(jnp.int32, s.shape, 0) // tile % steps
                token = lax.broadcasted_iota(jnp.int32, s.shape, 1)
                new.append(jnp.where(token <= step, s, NEG))
            return scores + [jnp.concatenate(x, axis=0) for x in (old, new)]

        def finish(task, scores):
            first = task * (BLOCK // per)
            m = functools.reduce(
                jnp.maximum, [jnp.max(s, axis=1, keepdims=True) for s in scores]
            )
            weights = [jnp.exp2((s - m) * SCALE2) for s in scores]
            l = sum(jnp.sum(p, axis=1, keepdims=True) for p in weights)
            probs = [p.astype(jnp.bfloat16) for p in weights]
            acc = dot_nt(probs[0], keys[:LATENT])
            new_probs = probs[2].astype(jnp.float32)
            for i in range(BLOCK // per):
                here = slice(i * per, (i + 1) * per)
                part = acc[here] + dot_nt(probs[1][here], suf_buf[first + i, :LATENT])
                values = new_buf[first + i][:, :LATENT].astype(jnp.float32)
                for t in range(steps):
                    part += new_probs[here, t : t + 1] * values[t : t + 1]
                there = pl.ds((first + i) * steps, steps)
                lead = (units, steps, tile)
                m_ref[:, there] = jnp.broadcast_to(m[here], (per, 128)).reshape(lead + (128,))
                l_ref[:, there] = jnp.broadcast_to(l[here], (per, 128)).reshape(lead + (128,))
                acc_ref[:, there] = part.reshape(lead + (LATENT,))

        in_turn(rows * per // BLOCK, score, finish, True)

    vmem, smem = pl.BlockSpec(memory_space=pltpu.VMEM), pl.BlockSpec(memory_space=pltpu.SMEM)
    lead = (units, rows * steps, tile)
    f32 = jnp.float32
    return call(
        body,
        [paused, suffix_len, queries, suffix_t, new_latent, own],
        [vmem, smem] + [vmem] * 4,
        [
            jax.ShapeDtypeStruct(lead + (width,), queries.dtype),
            jax.ShapeDtypeStruct(lead + (128,), f32),
            jax.ShapeDtypeStruct(lead + (128,), f32),
            jax.ShapeDtypeStruct(lead + (LATENT,), f32),
        ],
        [],
        bring,
        NEAR_LIMIT,
        rows * per * 1100 * 768,
        "near_attention",
    )


def merge(first, size, keys, q_ref, m_ref, l_ref, acc_ref, store, looped):
    _, pairs, tile, width = q_ref.shape
    step = BLOCK // tile
    blocks = pairs // step

    def at(task):
        return first + task // blocks, pl.ds(task % blocks * step, step)

    def score(task):
        here = at(task)
        q = q_ref[here].reshape(BLOCK, width)
        return [dot_nn(q, k) for k in keys]

    def finish(task, scores):
        here = at(task)
        store(
            task,
            here,
            *update(
                scores,
                m_ref[here].reshape(BLOCK, 128)[:, 0:1],
                l_ref[here].reshape(BLOCK, 128)[:, 0:1],
                acc_ref[here].reshape(BLOCK, LATENT),
                lambda acc, ps: acc + sum(dot_nt(p, k[:LATENT]) for p, k in zip(ps, keys)),
            ),
        )

    in_turn(size * blocks, score, finish, looped)


def middle_call(units, queries, state, keys, bring):
    _, pairs, tile, _ = queries.shape

    def body(ins, outs, _):
        q_ref, m_ref, l_ref, acc_ref, *key_refs = ins
        m_out, l_out, acc_out = outs

        def store(task, here, m, l, acc):
            lead = (BLOCK // tile, tile)
            m_out[here] = jnp.broadcast_to(m, (BLOCK, 128)).reshape(lead + (128,))
            l_out[here] = jnp.broadcast_to(l, (BLOCK, 128)).reshape(lead + (128,))
            acc_out[here] = acc.reshape(lead + (LATENT,))

        merge(0, units, [k[...] for k in key_refs], q_ref, m_ref, l_ref, acc_ref, store, bool(bring[1]))

    operands = [queries, *state, *keys]
    return call(
        body,
        operands,
        [pl.BlockSpec(memory_space=pltpu.VMEM)] * len(operands),
        [jax.ShapeDtypeStruct((units,) + x.shape[1:], x.dtype) for x in state],
        [],
        bring,
        28 if bring[1] else 10,
        2 * units * pairs * tile * 1100 * 256 * len(keys),
        "middle_attention",
    )


def far_call(first, size, queries, state, keys, axis_size, bring):
    _, pairs, tile, _ = queries.shape
    per_unit = pairs * tile

    def body(ins, out_refs, scratch):
        q_ref, m_ref, l_ref, acc_ref, *key_refs = ins
        (done,) = scratch

        me = lax.axis_index("roll")

        def part(u):
            for k in range(axis_size):
                there = u * per_unit + jnp.bitwise_xor(me, k) * CHUNK_HEADS
                for i in range(CHUNK_HEADS):
                    at = pl.ds(pl.multiple_of((u * CHUNK_HEADS + i) * pairs, pairs), pairs)
                    for g in range(LATENT // 128):
                        out_refs[k][at, g * 128 : (g + 1) * 128] = done[
                            g, pl.ds(there + i, pairs, stride=tile), :
                        ].astype(jnp.bfloat16)

        def store(task, here, m, l, acc):
            attended = acc * (1.0 / l)
            rows = pl.ds(task * BLOCK, BLOCK)
            for g in range(LATENT // 128):
                done[g, rows, :] = attended[:, g * 128 : (g + 1) * 128]
            if per_unit == BLOCK:
                part(task)

        keys_now = [k[...] for k in key_refs]
        merge(first, size, keys_now, q_ref, m_ref, l_ref, acc_ref, store, bool(bring[1]))
        if per_unit != BLOCK:
            for u in range(size):
                part(u)

    operands = [queries, *state, *keys]
    return call(
        body,
        operands,
        [pl.BlockSpec(memory_space=pltpu.VMEM)] * len(operands),
        [jax.ShapeDtypeStruct((size * CHUNK_HEADS * pairs, LATENT), jnp.bfloat16)] * axis_size,
        [pltpu.VMEM((LATENT // 128, size * per_unit + tile, 128), jnp.float32)],
        bring,
        FAR_LIMIT if bring[1] else 8,
        2 * size * per_unit * 1100 * 256 * len(keys),
        "far_attention",
    )


def project(first_head, heads, pieces, acc, w_uv, w_pieces, bring, kept=None, first_col=0, cols=None):
    pairs = pieces[0].shape[0] // heads
    total_rows = len(pieces) * pairs
    cols = w_pieces[0].shape[1] if cols is None else cols
    block = next(b for b in (1792, 1024, 896, 512, 128) if cols % b == 0)

    def body(ins, outs, _):
        ins = list(ins)
        piece_refs = [ins.pop(0) for _ in pieces]
        acc_ref = ins.pop(0) if acc is not None else None
        uv_ref, *w_refs = ins
        head_out = []
        for i in range(heads):
            rows = jnp.concatenate([p[i * pairs : (i + 1) * pairs, :] for p in piece_refs], axis=0)
            head_out.append(dot_nn(rows, uv_ref[first_head + i]).astype(jnp.bfloat16))
        head_out = jnp.concatenate(head_out, axis=1)

        def block_of(b):
            here = pl.ds(b * block, block)
            there = pl.ds(first_col + b * block, block)
            total, at = 0.0, 0
            for w_ref in w_refs:
                for row in range(0, w_ref.shape[0], K_STEP):
                    rows = slice(row, row + K_STEP)
                    total += dot_nn(head_out[:, at : at + K_STEP], w_ref[rows, there])
                    at += K_STEP
            if acc_ref is not None:
                total += acc_ref[:, there]
            if kept is None:
                outs[0][:, here] = total
                return
            at = [0, 0]
            for k in range(len(pieces)):
                side = 0 if k in kept else 1
                outs[side][at[side] * pairs : (at[side] + 1) * pairs, here] = total[
                    k * pairs : (k + 1) * pairs
                ].astype(jnp.bfloat16)
                at[side] += 1

        if bring[1]:
            pl.loop(0, cols // block)(block_of)
        else:
            for b in range(cols // block):
                block_of(b)

    operands = [*pieces] + ([acc] if acc is not None else []) + [w_uv, *w_pieces]
    if kept is not None:
        out_shape = [jax.ShapeDtypeStruct((total_rows // 2, cols), jnp.bfloat16)] * 2
    else:
        out_shape = [jax.ShapeDtypeStruct((total_rows, cols), jnp.float32)]
    return call(
        body,
        operands,
        [pl.BlockSpec(memory_space=pltpu.VMEM)] * len(operands),
        out_shape,
        [],
        bring,
        PROJECT_LIMIT if bring[1] else 8,
        8 * total_rows * heads * w_uv.shape[2] * cols,
        "project",
        {len(pieces): 0} if acc is not None and kept is None else {},
    )


def last_sums(shape, first_col, terms, so_far):
    rows, steps, _ = shape
    pairs = rows * steps
    cols = terms[0][0].shape[1]

    def kernel(*refs):
        out_ref, buf, sem = refs[-3:]
        total = None
        for ref, (_, first) in zip(refs, terms):
            x = ref[first : first + pairs, :].astype(jnp.float32)
            total = x if total is None else total + x
        buf[...] = total.astype(jnp.bfloat16).reshape(rows, steps, cols)
        copy = pltpu.make_async_copy(buf, out_ref.at[:, :, pl.ds(first_col, cols)], sem)
        copy.start()
        copy.wait()

    vmem, hbm = pl.BlockSpec(memory_space=pltpu.VMEM), pl.BlockSpec(memory_space=pltpu.HBM)
    held = [] if so_far is None else [so_far]
    return pl.pallas_call(
        kernel,
        in_specs=[vmem] * len(terms) + [hbm] * len(held),
        out_specs=hbm,
        out_shape=jax.ShapeDtypeStruct(shape, jnp.bfloat16),
        scratch_shapes=[pltpu.VMEM((rows, steps, cols), jnp.bfloat16), pltpu.SemaphoreType.DMA],
        input_output_aliases={len(terms): 0} if held else {},
        compiler_params=pltpu.CompilerParams(vmem_limit_bytes=8 * MIB),
        name="last_sums",
    )(*[x for x, _ in terms], *held)


def on_device(prefix_latent, suffix_latent, suffix_len, new_latent, queries, w_uv, w_out):
    n = lax.axis_size("roll")
    rows, steps, heads, _ = queries.shape
    pairs = rows * steps
    width = w_out.shape[1]
    share = heads // n
    units = share // CHUNK_HEADS
    chunks = [(0, units // 2), (units // 2, units - units // 2)] if units > 1 else [(0, 1)]
    depth = w_out.shape[0]
    half, eighth = depth // 2, depth // 8
    if len(chunks) > 1:
        brings = {
            "near": [(0, half - eighth)],
            ("far", 1): [(half - eighth, eighth)],
            ("project", 0): [(half, depth - half)],
        }
    else:
        brings = {"near": [(0, half)], "middle": [(half, depth - half)]}
    held = {}

    def bring(who):
        return (w_out, brings.get(who, []))

    def keep(who, result):
        out, brought = result
        held.update(zip(brings.get(who, []), brought))
        return out

    def swap(x, k):
        return lax.ppermute(x, "roll", [(i, i ^ k) for i in range(n)])

    own = prefix_latent.T.astype(jnp.bfloat16)
    own, paused = lax.optimization_barrier((own, pause()))
    across = [swap(own, k) for k in range(2, n, 2)]
    beside = swap(own, 1)
    queries, m, l, acc = keep(
        "near",
        near_call(
            paused,
            suffix_len,
            queries,
            jnp.swapaxes(suffix_latent, 1, 2),
            new_latent,
            own,
            units,
            n,
            bring("near"),
        ),
    )
    *across, m = lax.optimization_barrier((*across, m))
    forwarded = [swap(x, 1) for x in across]
    state = (m, l, acc)
    middle = keep("middle", middle_call(chunks[0][1], queries, state, [beside] + across, bring("middle")))
    got = []
    for c, (first, size) in enumerate(chunks):
        who = ("far", c)
        if c == 0:
            result = far_call(first, size, queries, middle, forwarded, n, bring(who))
        else:
            result = far_call(first, size, queries, state, [beside] + across + forwarded, n, bring(who))
        mine = keep(who, result)
        *mine, queries = lax.optimization_barrier((*mine, queries))
        if c == 1:
            *mine, late = lax.optimization_barrier((*mine, late))
            got[0][1] = swap(late, 1)
        got.append([mine[0]] + [None] * (n - 1))
        for k in [*range(2, n), 1]:
            if k == 1 and c == 0 and len(chunks) > 1:
                late = mine[1]
            else:
                got[c][k] = swap(mine[k], k)
    acc = None

    def pieces_of(first, size):
        unit_rows = depth // units
        first, end = first * unit_rows, (first + size) * unit_rows
        return [held[piece] for piece in sorted(held) if first <= piece[0] < end]

    for c, (first, size) in enumerate(chunks[:-1]):
        who = ("project", c)
        (acc,) = keep(
            who,
            project(
                first * CHUNK_HEADS,
                size * CHUNK_HEADS,
                got[c],
                acc,
                w_uv,
                pieces_of(first, size),
                bring(who),
            ),
        )
    first, size = chunks[-1]
    cols = width // OUT_PARTS
    parts = []
    for part in range(OUT_PARTS):
        odd = part % 2
        kept = tuple(k for k in range(n) if k == 0 or (k != 1 and k % 2 == odd))
        (stay, send), _ = project(
            first * CHUNK_HEADS,
            size * CHUNK_HEADS,
            got[-1],
            acc,
            w_uv,
            pieces_of(first, size),
            bring(None),
            kept,
            part * cols,
            cols,
        )
        left = [k for k in range(n) if k not in kept]
        recv = swap(send, 1)

        def piece(x, i):
            return x[i * pairs : (i + 1) * pairs].astype(jnp.float32)

        terms = [(stay, 0), (recv, left.index(1) * pairs)]
        for i, k in enumerate(kept[1:]):
            both = piece(stay, i + 1) + piece(recv, left.index(k ^ 1))
            terms.append((swap(both.astype(jnp.bfloat16), k), 0))
        parts.append(terms)
    out = None
    for part, terms in enumerate(parts):
        out = last_sums((rows, steps, width), part * cols, terms, out)
    return out


def solution(mesh):
    in_specs = (
        P(("group", "roll"), None),
        P(("group", "roll"), None, None),
        P(("group", "roll")),
        P(("group", "roll"), None, None),
        P(("group", "roll"), None, None, None),
        P("roll", None, None),
        P("roll", None),
    )
    out_specs = P(("group", "roll"), None, None)
    return jax.shard_map(
        on_device, mesh=mesh, in_specs=in_specs, out_specs=out_specs, check_vma=False
    )
```

```python
import functools
import math

import jax
import jax.numpy as jnp
from jax import lax
from jax.experimental import pallas as pl
from jax.experimental.pallas import tpu as pltpu
from jax.sharding import PartitionSpec as P

LATENT = 512
QK_HEAD = 192
SCALE2 = QK_HEAD**-0.5 * math.log2(math.e)
NEG = -1e30
CHUNK_HEADS = 4
OUT_PARTS = 2
BLOCK = 256
K_STEP = 256
MIB = 2**20
NEAR_LIMIT = 20
FAR_LIMIT = 20
PROJECT_LIMIT = 10
PAUSE_FLOPS = 10**10
PAUSE_BYTES = 30 * MIB


def dot_nt(a, b):
    return lax.dot_general(a, b, (((1,), (1,)), ((), ())), preferred_element_type=jnp.float32)


def dot_nn(a, b):
    return jnp.dot(a, b, preferred_element_type=jnp.float32)


def pause():
    def kernel(out_ref):
        out_ref[...] = jnp.zeros_like(out_ref)

    return pl.pallas_call(
        kernel,
        out_specs=pl.BlockSpec(memory_space=pltpu.VMEM),
        out_shape=pltpu.VMEM((8, 128), jnp.float32),
        cost_estimate=pl.CostEstimate(
            flops=PAUSE_FLOPS, bytes_accessed=PAUSE_BYTES, transcendentals=0
        ),
        name="pause",
    )()


def call(body, operands, in_specs, out_shape, scratch, bring, limit, flops, name, aliases=None):
    w_out, pieces = bring
    vmem, hbm = pl.BlockSpec(memory_space=pltpu.VMEM), pl.BlockSpec(memory_space=pltpu.HBM)
    n_in, n_out = len(operands), len(out_shape)
    copied = 0
    if pieces:
        operands, in_specs = [*operands, w_out], [*in_specs, hbm]
        out_shape = [*out_shape]
        out_shape += [pltpu.VMEM((count, w_out.shape[1]), w_out.dtype) for _, count in pieces]
        scratch = [*scratch, pltpu.SemaphoreType.DMA((len(pieces),))]
        copied = 2 * sum(count for _, count in pieces) * w_out.shape[1]

    def kernel(*refs):
        ins, rest = refs[: len(operands)], refs[len(operands) :]
        outs, rest = rest[: len(out_shape)], rest[len(out_shape) :]
        copies = []
        for i, piece in enumerate(pieces):
            copies.append(pltpu.make_async_copy(ins[-1].at[pl.ds(*piece)], outs[n_out + i], rest[-1].at[i]))
        for copy in copies:
            copy.start()
        body(ins[:n_in], outs[:n_out], rest[: len(scratch) - bool(pieces)])
        for copy in copies:
            copy.wait()

    out = pl.pallas_call(
        kernel,
        in_specs=in_specs,
        out_specs=[vmem] * len(out_shape),
        out_shape=out_shape,
        scratch_shapes=scratch,
        compiler_params=pltpu.CompilerParams(vmem_limit_bytes=limit * MIB),
        cost_estimate=pl.CostEstimate(
            flops=flops, bytes_accessed=4 * MIB + copied, transcendentals=0
        ),
        input_output_aliases=aliases or {},
        name=name,
    )(*operands)
    return out[:n_out], list(out[n_out:])


def update(scores, m, l, acc, probs_into):
    new_m = m
    for s in scores:
        new_m = jnp.maximum(new_m, jnp.max(s, axis=1, keepdims=True))
    shrink = jnp.exp2((m - new_m) * SCALE2)
    weights = [jnp.exp2((s - new_m) * SCALE2) for s in scores]
    l = l * shrink
    for p in weights:
        l += jnp.sum(p, axis=1, keepdims=True)
    return new_m, l, probs_into(acc * shrink, [p.astype(jnp.bfloat16) for p in weights])


def in_turn(tasks, score, finish, looped):
    def some(first, count):
        before = None
        for i in range(count):
            task = first + i
            now = score(task)
            if before is not None:
                finish(*before)
            before = (task, now)
        finish(*before)

    if tasks % 2 or not looped:
        some(0, tasks)
    else:

        @pl.loop(0, 2)
        def _(i):
            some(i * (tasks // 2), tasks // 2)


def near_call(paused, suffix_len, queries, suffix_t, new_latent, own, units, axis_size, bring):
    rows, steps, heads, width = queries.shape
    tile = heads // units
    share = heads // axis_size
    per = steps * heads

    def body(ins, outs, _):
        _, len_buf, q_buf, suf_buf, new_buf, own_ref = ins
        qs_ref, m_ref, l_ref, acc_ref = outs
        keys = own_ref[...]

        def sort(r):
            by_unit = [[] for _ in range(units)]
            for s in range(steps):
                q = q_buf[r, s].astype(jnp.float32)
                for u in range(units):
                    picked = [
                        q[j * share + u * CHUNK_HEADS : j * share + (u + 1) * CHUNK_HEADS]
                        for j in range(axis_size)
                    ]
                    by_unit[u].append(jnp.concatenate(picked, axis=0).astype(jnp.bfloat16))
            for u in range(units):
                for s in range(steps):
                    qs_ref[u, r * steps + s] = by_unit[u][s]
            return jnp.concatenate([x for unit in by_unit for x in unit], axis=0)

        def score(task):
            first = task * (BLOCK // per)
            q = [sort(first + i) for i in range(BLOCK // per)]
            both = jnp.concatenate(q, axis=0)
            scores = [dot_nn(both, keys)]
            old, new = [], []
            for i, x in enumerate(q):
                s = dot_nn(x, suf_buf[first + i])
                at = lax.broadcasted_iota(jnp.int32, s.shape, 1)
                old.append(jnp.where(at < len_buf[first + i], s, NEG))
                s = dot_nt(x, new_buf[first + i])
                step = lax.broadcasted_iota(jnp.int32, s.shape, 0) // tile % steps
                token = lax.broadcasted_iota(jnp.int32, s.shape, 1)
                new.append(jnp.where(token <= step, s, NEG))
            return scores + [jnp.concatenate(x, axis=0) for x in (old, new)]

        def finish(task, scores):
            first = task * (BLOCK // per)
            m = functools.reduce(
                jnp.maximum, [jnp.max(s, axis=1, keepdims=True) for s in scores]
            )
            weights = [jnp.exp2((s - m) * SCALE2) for s in scores]
            l = sum(jnp.sum(p, axis=1, keepdims=True) for p in weights)
            probs = [p.astype(jnp.bfloat16) for p in weights]
            acc = dot_nt(probs[0], keys[:LATENT])
            new_probs = probs[2].astype(jnp.float32)
            for i in range(BLOCK // per):
                here = slice(i * per, (i + 1) * per)
                part = acc[here] + dot_nt(probs[1][here], suf_buf[first + i, :LATENT])
                values = new_buf[first + i][:, :LATENT].astype(jnp.float32)
                for t in range(steps):
                    part += new_probs[here, t : t + 1] * values[t : t + 1]
                there = pl.ds((first + i) * steps, steps)
                lead = (units, steps, tile)
                m_ref[:, there] = jnp.broadcast_to(m[here], (per, 128)).reshape(lead + (128,))
                l_ref[:, there] = jnp.broadcast_to(l[here], (per, 128)).reshape(lead + (128,))
                acc_ref[:, there] = part.reshape(lead + (LATENT,))

        in_turn(rows * per // BLOCK, score, finish, True)

    vmem, smem = pl.BlockSpec(memory_space=pltpu.VMEM), pl.BlockSpec(memory_space=pltpu.SMEM)
    lead = (units, rows * steps, tile)
    f32 = jnp.float32
    return call(
        body,
        [paused, suffix_len, queries, suffix_t, new_latent, own],
        [vmem, smem] + [vmem] * 4,
        [
            jax.ShapeDtypeStruct(lead + (width,), queries.dtype),
            jax.ShapeDtypeStruct(lead + (128,), f32),
            jax.ShapeDtypeStruct(lead + (128,), f32),
            jax.ShapeDtypeStruct(lead + (LATENT,), f32),
        ],
        [],
        bring,
        NEAR_LIMIT,
        rows * per * 1100 * 768,
        "near_attention",
    )


def merge(first, size, keys, q_ref, m_ref, l_ref, acc_ref, store, looped):
    _, pairs, tile, width = q_ref.shape
    step = BLOCK // tile
    blocks = pairs // step

    def at(task):
        return first + task // blocks, pl.ds(task % blocks * step, step)

    def score(task):
        here = at(task)
        q = q_ref[here].reshape(BLOCK, width)
        return [dot_nn(q, k) for k in keys]

    def finish(task, scores):
        here = at(task)
        store(
            task,
            here,
            *update(
                scores,
                m_ref[here].reshape(BLOCK, 128)[:, 0:1],
                l_ref[here].reshape(BLOCK, 128)[:, 0:1],
                acc_ref[here].reshape(BLOCK, LATENT),
                lambda acc, ps: acc + sum(dot_nt(p, k[:LATENT]) for p, k in zip(ps, keys)),
            ),
        )

    in_turn(size * blocks, score, finish, looped)


def middle_call(units, queries, state, keys, bring):
    _, pairs, tile, _ = queries.shape

    def body(ins, outs, _):
        q_ref, m_ref, l_ref, acc_ref, *key_refs = ins
        m_out, l_out, acc_out = outs

        def store(task, here, m, l, acc):
            lead = (BLOCK // tile, tile)
            m_out[here] = jnp.broadcast_to(m, (BLOCK, 128)).reshape(lead + (128,))
            l_out[here] = jnp.broadcast_to(l, (BLOCK, 128)).reshape(lead + (128,))
            acc_out[here] = acc.reshape(lead + (LATENT,))

        merge(0, units, [k[...] for k in key_refs], q_ref, m_ref, l_ref, acc_ref, store, bool(bring[1]))

    operands = [queries, *state, *keys]
    return call(
        body,
        operands,
        [pl.BlockSpec(memory_space=pltpu.VMEM)] * len(operands),
        [jax.ShapeDtypeStruct((units,) + x.shape[1:], x.dtype) for x in state],
        [],
        bring,
        28 if bring[1] else 10,
        2 * units * pairs * tile * 1100 * 256 * len(keys),
        "middle_attention",
    )


def far_call(first, size, queries, state, keys, axis_size, bring):
    _, pairs, tile, _ = queries.shape
    per_unit = pairs * tile

    def body(ins, out_refs, scratch):
        q_ref, m_ref, l_ref, acc_ref, *key_refs = ins
        (done,) = scratch

        me = lax.axis_index("roll")

        def part(u):
            for k in range(axis_size):
                there = u * per_unit + jnp.bitwise_xor(me, k) * CHUNK_HEADS
                for i in range(CHUNK_HEADS):
                    at = pl.ds(pl.multiple_of((u * CHUNK_HEADS + i) * pairs, pairs), pairs)
                    for g in range(LATENT // 128):
                        out_refs[k][at, g * 128 : (g + 1) * 128] = done[
                            g, pl.ds(there + i, pairs, stride=tile), :
                        ].astype(jnp.bfloat16)

        def store(task, here, m, l, acc):
            attended = acc * (1.0 / l)
            rows = pl.ds(task * BLOCK, BLOCK)
            for g in range(LATENT // 128):
                done[g, rows, :] = attended[:, g * 128 : (g + 1) * 128]
            if per_unit == BLOCK:
                part(task)

        keys_now = [k[...] for k in key_refs]
        if len(keys) <= 3:
            keys_now = [jnp.concatenate(keys_now, axis=1)]
        merge(first, size, keys_now, q_ref, m_ref, l_ref, acc_ref, store, bool(bring[1]))
        if per_unit != BLOCK:
            for u in range(size):
                part(u)

    operands = [queries, *state, *keys]
    return call(
        body,
        operands,
        [pl.BlockSpec(memory_space=pltpu.VMEM)] * len(operands),
        [jax.ShapeDtypeStruct((size * CHUNK_HEADS * pairs, LATENT), jnp.bfloat16)] * axis_size,
        [pltpu.VMEM((LATENT // 128, size * per_unit + tile, 128), jnp.float32)],
        bring,
        FAR_LIMIT if bring[1] else 8,
        2 * size * per_unit * 1100 * 256 * len(keys),
        "far_attention",
    )


def project(first_head, heads, pieces, acc, w_uv, w_pieces, bring, kept=None, first_col=0, cols=None):
    pairs = pieces[0].shape[0] // heads
    total_rows = len(pieces) * pairs
    cols = w_pieces[0].shape[1] if cols is None else cols
    block = next(b for b in (1792, 1024, 896, 512, 128) if cols % b == 0)

    def body(ins, outs, _):
        ins = list(ins)
        piece_refs = [ins.pop(0) for _ in pieces]
        acc_ref = ins.pop(0) if acc is not None else None
        uv_ref, *w_refs = ins
        head_out = []
        for i in range(heads):
            rows = jnp.concatenate([p[i * pairs : (i + 1) * pairs, :] for p in piece_refs], axis=0)
            head_out.append(dot_nn(rows, uv_ref[first_head + i]).astype(jnp.bfloat16))
        head_out = jnp.concatenate(head_out, axis=1)

        def block_of(b):
            here = pl.ds(b * block, block)
            there = pl.ds(first_col + b * block, block)
            total, at = 0.0, 0
            for w_ref in w_refs:
                for row in range(0, w_ref.shape[0], K_STEP):
                    rows = slice(row, row + K_STEP)
                    total += dot_nn(head_out[:, at : at + K_STEP], w_ref[rows, there])
                    at += K_STEP
            if acc_ref is not None:
                total += acc_ref[:, there]
            if kept is None:
                outs[0][:, here] = total
                return
            at = [0, 0]
            for k in range(len(pieces)):
                side = 0 if k in kept else 1
                outs[side][at[side] * pairs : (at[side] + 1) * pairs, here] = total[
                    k * pairs : (k + 1) * pairs
                ].astype(jnp.bfloat16)
                at[side] += 1

        if bring[1]:
            pl.loop(0, cols // block)(block_of)
        else:
            for b in range(cols // block):
                block_of(b)

    operands = [*pieces] + ([acc] if acc is not None else []) + [w_uv, *w_pieces]
    if kept is not None:
        out_shape = [jax.ShapeDtypeStruct((total_rows // 2, cols), jnp.bfloat16)] * 2
    else:
        out_shape = [jax.ShapeDtypeStruct((total_rows, cols), jnp.float32)]
    return call(
        body,
        operands,
        [pl.BlockSpec(memory_space=pltpu.VMEM)] * len(operands),
        out_shape,
        [],
        bring,
        PROJECT_LIMIT if bring[1] else 8,
        8 * total_rows * heads * w_uv.shape[2] * cols,
        "project",
        {len(pieces): 0} if acc is not None and kept is None else {},
    )


def last_sums(shape, first_col, terms, so_far):
    rows, steps, _ = shape
    pairs = rows * steps
    cols = terms[0][0].shape[1]

    def kernel(*refs):
        out_ref, buf, sem = refs[-3:]
        total = None
        for ref, (_, first) in zip(refs, terms):
            x = ref[first : first + pairs, :].astype(jnp.float32)
            total = x if total is None else total + x
        buf[...] = total.astype(jnp.bfloat16).reshape(rows, steps, cols)
        copy = pltpu.make_async_copy(buf, out_ref.at[:, :, pl.ds(first_col, cols)], sem)
        copy.start()
        copy.wait()

    vmem, hbm = pl.BlockSpec(memory_space=pltpu.VMEM), pl.BlockSpec(memory_space=pltpu.HBM)
    held = [] if so_far is None else [so_far]
    return pl.pallas_call(
        kernel,
        in_specs=[vmem] * len(terms) + [hbm] * len(held),
        out_specs=hbm,
        out_shape=jax.ShapeDtypeStruct(shape, jnp.bfloat16),
        scratch_shapes=[pltpu.VMEM((rows, steps, cols), jnp.bfloat16), pltpu.SemaphoreType.DMA],
        input_output_aliases={len(terms): 0} if held else {},
        compiler_params=pltpu.CompilerParams(vmem_limit_bytes=8 * MIB),
        name="last_sums",
    )(*[x for x, _ in terms], *held)


def on_device(prefix_latent, suffix_latent, suffix_len, new_latent, queries, w_uv, w_out):
    n = lax.axis_size("roll")
    rows, steps, heads, _ = queries.shape
    pairs = rows * steps
    width = w_out.shape[1]
    share = heads // n
    units = share // CHUNK_HEADS
    chunks = [(0, units // 2), (units // 2, units - units // 2)] if units > 1 else [(0, 1)]
    depth = w_out.shape[0]
    half, eighth = depth // 2, depth // 8
    if len(chunks) > 1:
        brings = {
            "near": [(0, half - eighth)],
            ("far", 1): [(half - eighth, eighth)],
            ("project", 0): [(half, depth - half)],
        }
    else:
        brings = {"near": [(0, half)], "middle": [(half, depth - half)]}
    held = {}

    def bring(who):
        return (w_out, brings.get(who, []))

    def keep(who, result):
        out, brought = result
        held.update(zip(brings.get(who, []), brought))
        return out

    def swap(x, k):
        return lax.ppermute(x, "roll", [(i, i ^ k) for i in range(n)])

    own = prefix_latent.T.astype(jnp.bfloat16)
    own, paused = lax.optimization_barrier((own, pause()))
    across = [swap(own, k) for k in range(2, n, 2)]
    beside = swap(own, 1)
    queries, m, l, acc = keep(
        "near",
        near_call(
            paused,
            suffix_len,
            queries,
            jnp.swapaxes(suffix_latent, 1, 2),
            new_latent,
            own,
            units,
            n,
            bring("near"),
        ),
    )
    *across, m = lax.optimization_barrier((*across, m))
    forwarded = [swap(x, 1) for x in across]
    state = (m, l, acc)
    middle = keep("middle", middle_call(chunks[0][1], queries, state, [beside] + across, bring("middle")))
    got = []
    for c, (first, size) in enumerate(chunks):
        who = ("far", c)
        if c == 0:
            result = far_call(first, size, queries, middle, forwarded, n, bring(who))
        else:
            result = far_call(first, size, queries, state, [beside] + across + forwarded, n, bring(who))
        mine = keep(who, result)
        *mine, queries = lax.optimization_barrier((*mine, queries))
        if c == 1:
            *mine, late = lax.optimization_barrier((*mine, late))
            got[0][1] = swap(late, 1)
        got.append([mine[0]] + [None] * (n - 1))
        for k in [*range(2, n), 1]:
            if k == 1 and c == 0 and len(chunks) > 1:
                late = mine[1]
            else:
                got[c][k] = swap(mine[k], k)
    acc = None

    def pieces_of(first, size):
        unit_rows = depth // units
        first, end = first * unit_rows, (first + size) * unit_rows
        return [held[piece] for piece in sorted(held) if first <= piece[0] < end]

    for c, (first, size) in enumerate(chunks[:-1]):
        who = ("project", c)
        (acc,) = keep(
            who,
            project(
                first * CHUNK_HEADS,
                size * CHUNK_HEADS,
                got[c],
                acc,
                w_uv,
                pieces_of(first, size),
                bring(who),
            ),
        )
    first, size = chunks[-1]
    cols = width // OUT_PARTS
    parts = []
    for part in range(OUT_PARTS):
        odd = part % 2
        kept = tuple(k for k in range(n) if k == 0 or (k != 1 and k % 2 == odd))
        (stay, send), _ = project(
            first * CHUNK_HEADS,
            size * CHUNK_HEADS,
            got[-1],
            acc,
            w_uv,
            pieces_of(first, size),
            bring(None),
            kept,
            part * cols,
            cols,
        )
        left = [k for k in range(n) if k not in kept]
        recv = swap(send, 1)

        def piece(x, i):
            return x[i * pairs : (i + 1) * pairs].astype(jnp.float32)

        terms = [(stay, 0), (recv, left.index(1) * pairs)]
        for i, k in enumerate(kept[1:]):
            both = piece(stay, i + 1) + piece(recv, left.index(k ^ 1))
            terms.append((swap(both.astype(jnp.bfloat16), k), 0))
        parts.append(terms)
    out = None
    for part, terms in enumerate(parts):
        out = last_sums((rows, steps, width), part * cols, terms, out)
    return out


def solution(mesh):
    in_specs = (
        P(("group", "roll"), None),
        P(("group", "roll"), None, None),
        P(("group", "roll")),
        P(("group", "roll"), None, None),
        P(("group", "roll"), None, None, None),
        P("roll", None, None),
        P("roll", None),
    )
    out_specs = P(("group", "roll"), None, None)
    return jax.shard_map(
        on_device, mesh=mesh, in_specs=in_specs, out_specs=out_specs, check_vma=False
    )
```
